32 devices in a mesh: rep: 2 (over x), shard: 16 (over z, y, core).
Axes of the slice: x: 2, y: 2, z: 4, core: 2. Of those that a mesh axis runs over, the one named last changes fastest.
Arguments:
- row_ids: int32 [32768, 16, 4, 2], P(('rep', 'shard')), may hold values from 0 to 1023, as said below
- bag_lengths: int32 [32768, 16], P(('rep', 'shard')), may hold values from 3 to 4
- sample_counts: int32 [32], replicated, may hold values from 1 to 1024, as said below
- label_mask: int32 [32768, 5], P(('rep', 'shard')), may hold values 0 or 1
- labels: int32 [32768, 5], P(('rep', 'shard')), may hold values 0 or 1
- tables: float32 [262144, 128], P('shard'), may hold values from -4 to 4
- table_m: float32 [262144, 128], P('shard'), may hold values from -4.7683716e-07 to 4.7683716e-07
- table_v: float32 [262144, 128], P('shard'), may hold values from 4.8894437e-16 to 1.9790605e-15
- expert_w: float32 [8, 1024, 512], P(None, 'shard'), may hold values from -0.1875 to 0.1875
- expert_m: float32 [8, 1024, 512], P(None, 'shard'), may hold values from -1.9073486e-05 to 1.9073486e-05
- expert_v: float32 [8, 1024, 512], P(None, 'shard'), may hold values from 8.850098e-13 to 3.6621092e-12
- gate_w: float32 [1024, 40], P('shard'), may hold values from -0.09375 to 0.09375
- gate_m: float32 [1024, 40], P('shard'), may hold values from -0.00024414062 to 0.00024414062
- gate_v: float32 [1024, 40], P('shard'), may hold values from 1.14440915e-10 to 4.5776366e-10
- tower_weight_matrix: float32 [5, 512, 64], P(None, 'shard'), may hold values from -0.25 to 0.25
- tower_m: float32 [5, 512, 64], P(None, 'shard'), may hold values from -0.00021362305 to 0.00021362305
- tower_v: float32 [5, 512, 64], P(None, 'shard'), may hold values from 9.155274e-11 to 3.6621095e-10
- small_params: float32 [4741], replicated, may hold values from -1.5 to 1.5
- small_m: float32 [4741], replicated, may hold values from -1 to 1
- small_v: float32 [4741], replicated, may hold values from 0 to 1
Outputs:
- loss_parts: float32 [2], replicated
- table_new: float32 [262144, 128], P('shard')
- table_m_new: float32 [262144, 128], P('shard')
- table_v_new: float32 [262144, 128], P('shard')
- expert_new: float32 [8, 1024, 512], P(None, 'shard')
- expert_m_new: float32 [8, 1024, 512], P(None, 'shard')
- expert_v_new: float32 [8, 1024, 512], P(None, 'shard')
- gate_new: float32 [1024, 40], P('shard')
- gate_m_new: float32 [1024, 40], P('shard')
- gate_v_new: float32 [1024, 40], P('shard')
- tower_new: float32 [5, 512, 64], P(None, 'shard')
- tower_m_new: float32 [5, 512, 64], P(None, 'shard')
- tower_v_new: float32 [5, 512, 64], P(None, 'shard')
- small_new: float32 [4741], replicated
- small_m_new: float32 [4741], replicated
- small_v_new: float32 [4741], replicated
The draws below stay inside these ranges and needn't reach their ends.
Inputs may be any that keep to these rules, and one draw needn't show every extreme that they name: row_ids[..., 0] * 1024 + row_ids[..., 1] is a row number of 0 to 262143, and row_ids[..., 1] is under 1024. In the 65536 slots of each device's samples (used or not), every block of 16384 consecutive row numbers is named exactly 4096 times, 4096 / 2 times by bags of each table; among those slots of one device that name one block through one table, every row named is named exactly twice, so that they hold exactly 1024 distinct rows. `sample_counts`: entry d counts the samples that take part on device d (devices in the order of rep+shard); they are its first ones. The last device's count is 1024.
All inputs are finite; a program needn't handle non-finite values. No bound on the sum of `label_mask` or of `labels` on one device may be relied on, other than what follows from the above.
Results may differ from the reference program's by a relative error of at most 0.0074.
Values may be sent and summed in bfloat16 or wider, within the bound.
No kernel may reach another device: no remote copies, remote signals or barrier semaphores. Data moves between devices by JAX's collectives and lax.ppermute only.
A program may use at most 256 MiB of HBM per device.

```python
import math
import jax
import jax.numpy as jnp
from jax import lax

SAMP_DEV = 1024
BAGS = 16
TABLES = 2
WIDTH = 64
ROWS = 262144
ROW_BASE = 1024
LMAX = 4
EXPERTS = 8
HID = 512
TASKS = 5
TOWER = 64
STEP = 10
D_IN = 1024
SAMPLES = 32768
SMALL = 4741
N_REP = 2
N_SHARD = 16
DEVICES = 32


def small_scales():
    pieces = [jnp.full((EXPERTS * HID,), 0.0044, jnp.float32), jnp.full((TASKS * TOWER,), 0.075, jnp.float32), jnp.full((TASKS * TOWER,), 0.25, jnp.float32), jnp.full((TASKS,), 0.5, jnp.float32)]
    return jnp.concatenate(pieces) * jnp.sqrt(1.5 / (SAMP_DEV * DEVICES))


def draw_small_m(key, part):
    key = jax.random.fold_in(key, 11)
    return 0.111 * small_scales() * jax.random.normal(key, (SMALL,), jnp.float32)


def draw_small_v(key, part):
    key = jax.random.fold_in(key, 12)
    spread = jnp.exp(jax.random.uniform(key, (SMALL,), jnp.float32, 0.0, jnp.log(4.0)))
    scaled = small_scales()
    return 0.001 * spread * scaled * scaled


def draw_row_ids(key, part):
    key = jax.random.fold_in(key, 21)
    per_table = BAGS // TABLES
    table_slots = SAMP_DEV * per_table * LMAX
    rows_dev = ROWS // N_SHARD
    key_order, key_shift, key_shuffle = jax.random.split(key, 3)
    scores = jax.random.randint(key_order, (DEVICES, TABLES, table_slots), 0, 4096, jnp.int32) * table_slots
    scores = scores + jnp.arange(table_slots, dtype=jnp.int32)[None, None, :]
    places = jnp.argsort(scores, axis=2).astype(jnp.int32)
    owners = places % N_SHARD
    pair_index = places // N_SHARD // 2
    shifts = jax.random.randint(key_shift, (DEVICES, TABLES, N_SHARD), 0, rows_dev, jnp.int32)
    owner_shift = jnp.take_along_axis(shifts, owners, axis=2)
    shuffle_scores = jax.random.randint(key_shuffle, (DEVICES, TABLES, rows_dev), 0, 4096, jnp.int32) * rows_dev
    shuffle_scores = shuffle_scores + jnp.arange(rows_dev, dtype=jnp.int32)[None, None, :]
    shuffled = jnp.argsort(shuffle_scores, axis=2).astype(jnp.int32)
    position = ((pair_index + owner_shift) % rows_dev).astype(jnp.int32)
    offset = jnp.take_along_axis(shuffled, position, axis=2)
    row_values = (owners * rows_dev + offset).reshape(DEVICES, TABLES, SAMP_DEV, per_table, LMAX)
    row_values = jnp.transpose(row_values, (0, 2, 1, 3, 4)).reshape(SAMP_DEV * DEVICES, BAGS, LMAX)
    high_digit = row_values // ROW_BASE
    low_digit = row_values % ROW_BASE
    return jnp.stack([high_digit, low_digit], axis=-1).astype(jnp.int32)


def draw_sample_counts(key, part):
    key = jax.random.fold_in(key, 31)
    device = jnp.arange(DEVICES, dtype=jnp.int32)
    rep_pos = device // N_SHARD
    shard_pos = device % N_SHARD
    ascent = rep_pos * (N_SHARD - 1) + shard_pos * (N_REP - 1)
    summit = 2 * (N_REP - 1) * (N_SHARD - 1)
    low_base = SAMP_DEV // 3
    base_count = low_base + (SAMP_DEV - low_base) * ascent // summit
    jitter = jax.random.randint(key, (DEVICES,), 0, SAMP_DEV // 8 + 1, jnp.int32)
    counts = jnp.maximum(base_count - jitter, 1)
    return jnp.where(device == DEVICES - 1, SAMP_DEV, counts).astype(jnp.int32)


def touch_ends(entries, rng, low, top_value):
    longest = entries.shape.index(max(entries.shape))
    spots = []
    for shift in (0, 1):
        where = [jax.random.randint(jax.random.fold_in(rng, axis), (), 0, length) for axis, length in enumerate(entries.shape)]
        where[longest] = (where[longest] + shift) % entries.shape[longest]
        spots.append(tuple(where))
    return entries.at[spots[0]].set(low).at[spots[1]].set(top_value)


def shard_levels(own_key, extent, cuts, smallest, largest):
    def one(axis_at, parts):
        steps = jax.random.uniform(jax.random.fold_in(jax.random.fold_in(own_key, 6), axis_at), (parts,), jnp.float32, smallest / len(cuts), largest / len(cuts))
        return jnp.repeat(jnp.exp(steps), extent[axis_at] // parts).reshape((-1,) + (1,) * (len(extent) - axis_at - 1))

    gain = one(*cuts[0])
    for cut in cuts[1:]:
        gain = gain * one(*cut)
    return gain


def bell_draw(key, dims, deviation, reach, cuts=(), kind=jnp.bfloat16):
    level = shard_levels(key, dims, cuts, -0.22, 0.18) if cuts else 1.0
    result = jax.random.normal(key, dims, jnp.float32) * deviation * level
    return jnp.minimum(jnp.maximum(result, -reach), reach).astype(kind)


def setup_inputs(seed: int = 0) -> dict:
    streams_of = jax.random.split(jax.random.key(seed), 21)
    row_ids = draw_row_ids(jax.random.fold_in(streams_of[20], 71), 0)
    bag_lengths = touch_ends(jax.random.randint(streams_of[1], (SAMPLES, BAGS), 3, LMAX + 1), jax.random.fold_in(streams_of[1], 1), 3, LMAX).astype(jnp.int32)
    sample_counts = draw_sample_counts(jax.random.fold_in(streams_of[20], 71), 0)
    label_mask = touch_ends((jax.random.randint(streams_of[3], (SAMPLES, TASKS), 0, 5) < 4).astype(jnp.int32), jax.random.fold_in(streams_of[3], 1), 0, 1)
    labels = touch_ends((jax.random.randint(streams_of[4], (SAMPLES, TASKS), 0, 3) < 1).astype(jnp.int32), jax.random.fold_in(streams_of[4], 1), 0, 1)
    tables = bell_draw(streams_of[5], (ROWS, TABLES * WIDTH), 0.53, 4.0, ((0, 16),), jnp.float32)
    table_m = bell_draw(streams_of[6], (ROWS, TABLES * WIDTH), (0.0072 * (SAMP_DEV * DEVICES * ROWS) ** -0.5), 4.76837158203125e-07, ((0, 16),), jnp.float32)
    table_v = jnp.clip(jnp.exp(math.log(1.979060505765914e-15) - 1.3981288 * jax.random.uniform(streams_of[7], (ROWS, TABLES * WIDTH), jnp.float32) ** shard_levels(streams_of[7], (ROWS, TABLES * WIDTH), ((0, 16),), -0.2, 0.2)), 4.889443689675061e-16, 1.979060505765914e-15)
    expert_w = bell_draw(streams_of[8], (EXPERTS, D_IN, HID), D_IN ** -0.5, 0.1875, ((1, 16),), jnp.float32)
    expert_m = bell_draw(streams_of[9], (EXPERTS, D_IN, HID), (0.0006 * (SAMP_DEV * DEVICES) ** -0.5), 1.9073486328125e-05, ((1, 16),), jnp.float32)
    expert_v = jnp.clip(jnp.exp(math.log(3.662109244323419e-12) - 1.42019586 * jax.random.uniform(streams_of[10], (EXPERTS, D_IN, HID), jnp.float32) ** shard_levels(streams_of[10], (EXPERTS, D_IN, HID), ((1, 16),), -0.2, 0.2)), 8.850097846409277e-13, 3.662109244323419e-12)
    gate_w = bell_draw(streams_of[11], (D_IN, TASKS * EXPERTS), (0.5 * D_IN ** -0.5), 0.09375, ((0, 16),), jnp.float32)
    gate_m = bell_draw(streams_of[12], (D_IN, TASKS * EXPERTS), (0.0068 * (SAMP_DEV * DEVICES) ** -0.5), 0.00024414062, ((0, 16),), jnp.float32)
    gate_v = jnp.clip(jnp.exp(math.log(4.57763660310917e-10) - 1.3862944 * jax.random.uniform(streams_of[13], (D_IN, TASKS * EXPERTS), jnp.float32) ** shard_levels(streams_of[13], (D_IN, TASKS * EXPERTS), ((0, 16),), -0.2, 0.2)), 1.1444091507772924e-10, 4.57763660310917e-10)
    tower_weight_matrix = bell_draw(streams_of[14], (TASKS, HID, TOWER), HID ** -0.5, 0.25, ((1, 16),), jnp.float32)
    tower_m = bell_draw(streams_of[15], (TASKS, HID, TOWER), (0.0061 * (SAMP_DEV * DEVICES) ** -0.5), 0.00021362305, ((1, 16),), jnp.float32)
    tower_v = jnp.clip(jnp.exp(math.log(3.6621095045319407e-10) - 1.3862944 * jax.random.uniform(streams_of[16], (TASKS, HID, TOWER), jnp.float32) ** shard_levels(streams_of[16], (TASKS, HID, TOWER), ((1, 16),), -0.2, 0.2)), 9.155273761329852e-11, 3.6621095045319407e-10)
    small_params = bell_draw(streams_of[17], (SMALL,), 0.25, 1.5, (), jnp.float32)
    small_m = draw_small_m(jax.random.fold_in(streams_of[20], 71), 0)
    small_v = draw_small_v(jax.random.fold_in(streams_of[20], 71), 0)
    return dict(row_ids=row_ids, bag_lengths=bag_lengths, sample_counts=sample_counts, label_mask=label_mask, labels=labels, tables=tables, table_m=table_m, table_v=table_v, expert_w=expert_w, expert_m=expert_m, expert_v=expert_v, gate_w=gate_w, gate_m=gate_m, gate_v=gate_v, tower_weight_matrix=tower_weight_matrix, tower_m=tower_m, tower_v=tower_v, small_params=small_params, small_m=small_m, small_v=small_v)


@jax.custom_vjp
def reduced_precision(v):
    return lax.optimization_barrier(v.astype(jnp.bfloat16)).astype(jnp.float32)

@jax.custom_vjp
def reduced_backward(v):
    return v

def low_keep(v):
    return (reduced_precision(v), None)

def low_pass(kept, grad):
    return (grad,)

def back_keep(v):
    return (v, None)

def back_low(kept, grad):
    return (reduced_precision(grad),)
reduced_precision.defvjp(low_keep, low_pass)
reduced_backward.defvjp(back_keep, back_low)
beta_first = 0.9
beta_second = 0.999
adam_epsilon = 1e-08
weight_decay = 0.01
rate_table = 1.0
rate_expert = 0.06
rate_gate = 0.03
rate_tower = 0.08
rate_small = 0.5
top_precision = lax.Precision.HIGHEST

def swish(value):
    return value * jax.nn.sigmoid(value)

def adamw(weight, grad, first, second, rate):
    first_new = beta_first * first + (1.0 - beta_first) * grad
    second_new = beta_second * second + (1.0 - beta_second) * grad * grad
    first_hat = first_new / (1.0 - beta_first ** STEP)
    second_hat = second_new / (1.0 - beta_second ** STEP)
    weight_new = weight - rate * (first_hat / (jnp.sqrt(second_hat) + adam_epsilon) + weight_decay * weight)
    return (weight_new, first_new, second_new)

def unpack_small(small_params):
    first_end = EXPERTS * HID
    second_end = first_end + TASKS * TOWER
    third_end = second_end + TASKS * TOWER
    expert_bias = small_params[:first_end].reshape(EXPERTS, HID)
    tower_layer_bias = small_params[first_end:second_end].reshape(TASKS, TOWER)
    head_weight = small_params[second_end:third_end].reshape(TASKS, TOWER)
    head_bias = small_params[third_end:]
    return (expert_bias, tower_layer_bias, head_weight, head_bias)

def block_loss(params, row_block, length_block, live_block, label_block, sample_total):
    tables, expert_w, gate_w, tower_weight_matrix, small_params = params
    expert_bias, tower_layer_bias, head_weight, head_bias = unpack_small(small_params)
    samples_here = row_block.shape[0]
    table_view = tables.reshape(ROWS, TABLES, WIDTH)
    table_of = jnp.arange(BAGS, dtype=jnp.int32) // (BAGS // TABLES)
    looked = table_view[row_block, table_of[None, :, None]]
    used_mask = (jnp.arange(LMAX, dtype=jnp.int32)[None, None, :] < length_block[:, :, None]).astype(jnp.float32)
    pooled = lax.optimization_barrier(jnp.sum(reduced_precision(looked) * used_mask[..., None], axis=2)).reshape(samples_here, BAGS * WIDTH)
    pooled_low = reduced_precision(pooled)
    expert_pre = reduced_backward(jnp.einsum('sd,edh->esh', pooled_low, reduced_precision(expert_w), precision=top_precision) + expert_bias[:, None, :])
    expert_out = swish(expert_pre)
    gate_logits = reduced_backward(jnp.dot(pooled_low, reduced_precision(gate_w), precision=top_precision)).reshape(samples_here, TASKS, EXPERTS)
    gates = jax.nn.softmax(gate_logits, axis=-1)
    mixed_features = jnp.einsum('ske,esh->skh', gates, expert_out, precision=top_precision)
    tower_preactivation = reduced_backward(jnp.einsum('bme,meu->bmu', reduced_precision(mixed_features), reduced_precision(tower_weight_matrix), precision=top_precision) + tower_layer_bias[None])
    tower_out = swish(tower_preactivation)
    logit_out = lax.optimization_barrier(jnp.sum(tower_out * head_weight[None], axis=-1)) + head_bias[None]
    losses = jax.nn.softplus(logit_out) - label_block * logit_out
    raw_sum = jnp.sum(live_block * losses)
    return (raw_sum / sample_total, raw_sum)

def add_trees(left, right):
    return jax.tree.map(jnp.add, left, right)

def reference(row_ids, bag_lengths, sample_counts, label_mask, labels, tables, table_m, table_v, expert_w, expert_m, expert_v, gate_w, gate_m, gate_v, tower_weight_matrix, tower_m, tower_v, small_params, small_m, small_v):
    row_numbers = (row_ids[..., 0] * ROW_BASE + row_ids[..., 1]).astype(jnp.int32)
    sample_total = jnp.sum(sample_counts).astype(jnp.float32)
    positions = jnp.arange(SAMPLES, dtype=jnp.int32)
    limits = jnp.take(sample_counts, positions // SAMP_DEV)
    live_mask = (positions % SAMP_DEV < limits).astype(jnp.float32)[:, None] * label_mask.astype(jnp.float32)
    label_values = labels.astype(jnp.float32)
    block_size = math.gcd(SAMPLES, 4096)
    block_count = SAMPLES // block_size
    params = (tables, expert_w, gate_w, tower_weight_matrix, small_params)

    def step_block(carry, pieces):
        grads, loss_sum = carry
        row_block, length_block, live_block, label_block = pieces

        def loss_of(params_in):
            return block_loss(params_in, row_block, length_block, live_block, label_block, sample_total)
        value, pullback, raw_sum = jax.vjp(loss_of, params, has_aux=True)
        block_grads = pullback(jnp.ones_like(value))[0]
        return ((add_trees(grads, block_grads), loss_sum + raw_sum), None)
    zero_grads = jax.tree.map(jnp.zeros_like, params)
    pieces = (row_numbers.reshape(block_count, block_size, BAGS, LMAX), bag_lengths.reshape(block_count, block_size, BAGS), live_mask.reshape(block_count, block_size, TASKS), label_values.reshape(block_count, block_size, TASKS))
    (grads, loss_sum), unused = lax.scan(step_block, (zero_grads, jnp.zeros((), jnp.float32)), pieces)
    table_new, table_m_new, table_v_new = adamw(tables, grads[0], table_m, table_v, rate_table)
    expert_new, expert_m_new, expert_v_new = adamw(expert_w, grads[1], expert_m, expert_v, rate_expert)
    gate_new, gate_m_new, gate_v_new = adamw(gate_w, grads[2], gate_m, gate_v, rate_gate)
    tower_new, tower_m_new, tower_v_new = adamw(tower_weight_matrix, grads[3], tower_m, tower_v, rate_tower)
    small_new, small_m_new, small_v_new = adamw(small_params, grads[4], small_m, small_v, rate_small)
    loss_parts = jnp.stack([loss_sum, sample_total])
    return (loss_parts, table_new, table_m_new, table_v_new, expert_new, expert_m_new, expert_v_new, gate_new, gate_m_new, gate_v_new, tower_new, tower_m_new, tower_v_new, small_new, small_m_new, small_v_new)
```

```python
import functools

import jax
import jax.numpy as jnp
from jax import lax
from jax.experimental import pallas as pl
from jax.experimental.pallas import tpu as pltpu
from jax.sharding import PartitionSpec as P

TABLES = 2
WIDTH = 64
ROW_BASE = 1024
EXPERTS = 8
HID = 512
TASKS = 5
TOWER = 64
STEP = 10
LANES = 128
UNROLL = 16
VMEM_BYTES = 60 << 20

beta_first = 0.9
beta_second = 0.999
adam_epsilon = 1e-08
weight_decay = 0.01
rate_table = 1.0
rate_expert = 0.06
rate_gate = 0.03
rate_tower = 0.08
rate_small = 0.5


def adamw(weight, grad, first, second, rate):
    first_new = beta_first * first + (1.0 - beta_first) * grad
    second_new = beta_second * second + (1.0 - beta_second) * grad * grad
    first_hat = first_new / (1.0 - beta_first**STEP)
    second_hat = second_new / (1.0 - beta_second**STEP)
    weight_new = weight - rate * (
        first_hat / (jnp.sqrt(second_hat) + adam_epsilon) + weight_decay * weight
    )
    return (weight_new, first_new, second_new)


def left_lanes(rows=1):
    return lax.broadcasted_iota(jnp.int32, (rows, LANES), 1) < WIDTH


def params(**kw):
    return pltpu.CompilerParams(vmem_limit_bytes=VMEM_BYTES, **kw)


def owner_gather_kernel(distinct, want_ref, table_ref, out_ref, rows_ref):
    left = left_lanes()

    def body(step, carry):
        base = step * UNROLL
        for u in range(UNROLL):
            first = table_ref[pl.ds(want_ref[2 * (base + u)], 1), :]
            second = table_ref[pl.ds(want_ref[2 * (distinct + base + u)], 1), :]
            rows_ref[pl.ds(base + u, 1), :] = jnp.where(left, first, second)
        return carry

    lax.fori_loop(0, distinct // UNROLL, body, 0)
    out_ref[0] = rows_ref[...].astype(jnp.bfloat16)


def owner_gather(wanted, table, shards, distinct):
    rows = table.shape[0]
    return pl.pallas_call(
        functools.partial(owner_gather_kernel, distinct),
        name="owner_gather",
        grid=(shards,),
        in_specs=[
            pl.BlockSpec((4 * distinct,), lambda i: (i,), memory_space=pltpu.SMEM),
            pl.BlockSpec((rows, LANES), lambda i: (0, 0), pipeline_mode=pl.Buffered(1)),
        ],
        out_specs=pl.BlockSpec((1, distinct, LANES), lambda i: (i, 0, 0)),
        out_shape=jax.ShapeDtypeStruct((shards, distinct, LANES), jnp.bfloat16),
        scratch_shapes=[pltpu.VMEM((distinct, LANES), jnp.float32)],
        compiler_params=params(),
    )(wanted, table)


def pool_kernel(samples, longest, q0_ref, q1_ref, reply_ref, out_ref, rows_ref, sum_ref):
    count = reply_ref.shape[0]

    @pl.when(pl.program_id(0) == 0)
    def _():
        rows_ref[0:count, :] = reply_ref[...].astype(jnp.float32)
        rows_ref[count : count + 8, :] = jnp.zeros((8, LANES), jnp.float32)

    left = left_lanes()
    unroll = UNROLL // 4

    def summed(index_ref, s):
        total = rows_ref[pl.ds(index_ref[s], 1), :]
        for slot in range(1, longest):
            total = total + rows_ref[pl.ds(index_ref[slot * samples + s], 1), :]
        return total

    def body(step, carry):
        for u in range(unroll):
            s = step * unroll + u
            sum_ref[pl.ds(s, 1), :] = jnp.where(left, summed(q0_ref, s), summed(q1_ref, s))
        return carry

    lax.fori_loop(0, samples // unroll, body, 0)
    out_ref[0] = sum_ref[...].astype(jnp.bfloat16)


def pool(places, replies, samples, longest, pairs):
    count = replies.shape[0]
    return pl.pallas_call(
        functools.partial(pool_kernel, samples, longest),
        name="pool",
        grid=(pairs,),
        in_specs=[
            pl.BlockSpec((longest * samples,), lambda i: (i,), memory_space=pltpu.SMEM),
            pl.BlockSpec((longest * samples,), lambda i: (i + pairs,), memory_space=pltpu.SMEM),
            pl.BlockSpec((count, LANES), lambda i: (0, 0), pipeline_mode=pl.Buffered(1)),
        ],
        out_specs=pl.BlockSpec((1, samples, LANES), lambda i: (i, 0, 0)),
        out_shape=jax.ShapeDtypeStruct((pairs, samples, LANES), jnp.bfloat16),
        scratch_shapes=[
            pltpu.VMEM((count + 8, LANES), jnp.float32),
            pltpu.VMEM((samples, LANES), jnp.float32),
        ],
        compiler_params=params(),
    )(places, places, replies)


def grad_gather_kernel(distinct, index_ref, grad_ref, out_ref, grads_ref, rows_ref):
    count = grad_ref.shape[0]

    @pl.when(pl.program_id(0) == 0)
    def _():
        grads_ref[0:count, :] = grad_ref[...]
        grads_ref[count : count + 8, :] = jnp.zeros((8, LANES), jnp.float32)

    left = left_lanes()
    unroll = UNROLL // 2

    def both(at):
        first = grads_ref[pl.ds(index_ref[at], 1), :]
        return first + grads_ref[pl.ds(index_ref[at + 1], 1), :]

    def body(step, carry):
        for u in range(unroll):
            r = step * unroll + u
            rows_ref[pl.ds(r, 1), :] = jnp.where(left, both(2 * r), both(2 * (distinct + r)))
        return carry

    lax.fori_loop(0, distinct // unroll, body, 0)
    out_ref[0] = rows_ref[...].astype(jnp.bfloat16)


def grad_gather(index, grads, shards, distinct):
    count = grads.shape[0]
    return pl.pallas_call(
        functools.partial(grad_gather_kernel, distinct),
        name="grad_gather",
        grid=(shards,),
        in_specs=[
            pl.BlockSpec((4 * distinct,), lambda i: (i,), memory_space=pltpu.SMEM),
            pl.BlockSpec((count, LANES), lambda i: (0, 0), pipeline_mode=pl.Buffered(1)),
        ],
        out_specs=pl.BlockSpec((1, distinct, LANES), lambda i: (i, 0, 0)),
        out_shape=jax.ShapeDtypeStruct((shards, distinct, LANES), jnp.bfloat16),
        scratch_shapes=[
            pltpu.VMEM((count + 8, LANES), jnp.float32),
            pltpu.VMEM((distinct, LANES), jnp.float32),
        ],
        compiler_params=params(),
    )(index, grads)


def scatter_kernel(distinct, want_ref, got_ref, out_ref, sum0_ref, sum1_ref, rows_ref):

    @pl.when(pl.program_id(0) == 0)
    def _():
        sum0_ref[...] = jnp.zeros_like(sum0_ref)
        sum1_ref[...] = jnp.zeros_like(sum1_ref)

    rows_ref[...] = got_ref[0].astype(jnp.float32)

    def body(step, carry):
        base = step * UNROLL
        span = range(UNROLL)
        at0 = [want_ref[2 * (base + u)] for u in span]
        at1 = [want_ref[2 * (distinct + base + u)] for u in span]
        came = [rows_ref[pl.ds(base + u, 1), :] for u in span]
        new0 = [sum0_ref[pl.ds(at0[u], 1), :] + came[u] for u in span]
        new1 = [sum1_ref[pl.ds(at1[u], 1), :] + came[u] for u in span]
        for u in span:
            sum0_ref[pl.ds(at0[u], 1), :] = new0[u]
        for u in span:
            sum1_ref[pl.ds(at1[u], 1), :] = new1[u]
        return carry

    lax.fori_loop(0, distinct // UNROLL, body, 0)

    @pl.when(pl.program_id(0) == pl.num_programs(0) - 1)
    def _():
        out_ref[...] = jnp.where(left_lanes(), sum0_ref[...], sum1_ref[...]).astype(jnp.bfloat16)


def scatter(wanted, arrived, rows):
    shards, distinct = arrived.shape[:2]
    return pl.pallas_call(
        functools.partial(scatter_kernel, distinct),
        name="scatter",
        grid=(shards,),
        in_specs=[
            pl.BlockSpec((4 * distinct,), lambda i: (i,), memory_space=pltpu.SMEM),
            pl.BlockSpec((1, distinct, LANES), lambda i: (i, 0, 0)),
        ],
        out_specs=pl.BlockSpec((rows, LANES), lambda i: (0, 0)),
        out_shape=jax.ShapeDtypeStruct((rows, LANES), jnp.bfloat16),
        scratch_shapes=[
            pltpu.VMEM((rows, LANES), jnp.float32),
            pltpu.VMEM((rows, LANES), jnp.float32),
            pltpu.VMEM((distinct, LANES), jnp.float32),
        ],
        compiler_params=params(),
    )(wanted, arrived)


def group_reduce(value, op):
    lane = lax.broadcasted_iota(jnp.int32, value.shape, 1)
    shift = 1
    while shift < EXPERTS:
        other = jnp.where(
            (lane & shift) != 0,
            pltpu.roll(value, shift, 1),
            pltpu.roll(value, LANES - shift, 1),
        )
        value = op(value, other)
        shift *= 2
    return value


def tower_spot(k, depth):
    half = depth // 2
    return (0 if k < 3 else half), (k % 3 + 1) * LANES


def dense_kernel(
    shards,
    pooled_ref,
    weight_ref,
    bias_ref,
    tower_bias_ref,
    head_ref,
    head_bias_ref,
    live_ref,
    label_ref,
    scale_ref,
    grad_ref,
    expert_grad_ref,
    x_out_ref,
    gate_grad_ref,
    tower_grad_ref,
    small_ref,
    x_ref,
    out_ref,
    slope_ref,
    mixed_ref,
    mixed_grad_ref,
    gates_ref,
    gate_prob_ref,
    tower_ref,
):
    pairs = pooled_ref.shape[0]
    block = pooled_ref.shape[1]
    depth = weight_ref.shape[1] // shards
    half = depth // 2
    step = pl.program_id(0)

    @pl.when(step == 0)
    def _():
        for k in range(TASKS):
            row, col = tower_spot(k, depth)
            for i in range(shards):
                tower_ref[k, i * half : (i + 1) * half, :] = weight_ref[
                    EXPERTS, i * depth + row : i * depth + row + half, col : col + TOWER
                ]
        small_ref[...] = jnp.zeros_like(small_ref)
        tower_grad_ref[...] = jnp.zeros_like(tower_grad_ref)

    left = left_lanes(block)
    for m in range(pairs // 2):
        even = pooled_ref[2 * m].astype(jnp.float32)
        odd = pooled_ref[2 * m + 1].astype(jnp.float32)
        low = jnp.where(left, even, pltpu.roll(odd, WIDTH, 1)).astype(jnp.bfloat16)
        high = jnp.where(left, pltpu.roll(even, WIDTH, 1), odd).astype(jnp.bfloat16)
        x_ref[:, m * LANES : (m + 1) * LANES] = low
        high_at = (m + pairs // 2) * LANES
        x_ref[:, high_at : high_at + LANES] = high
    x_out_ref[...] = x_ref[...]

    logits = jnp.dot(
        x_ref[...], weight_ref[EXPERTS, :, 0:LANES], preferred_element_type=jnp.float32
    )
    top = group_reduce(logits, jnp.maximum)
    powers = jnp.exp(logits - top)
    gates_ref[...] = powers / group_reduce(powers, jnp.add)

    def expert(e, carry):
        pre = jnp.dot(x_ref[...], weight_ref[e], preferred_element_type=jnp.float32)
        pre = pre + bias_ref[e]
        sigma = jax.nn.sigmoid(pre)
        out = pre * sigma
        out_ref[e] = out
        slope_ref[e] = sigma + out * (1.0 - sigma)
        return carry

    lax.fori_loop(0, EXPERTS, expert, 0)

    def mix(c, carry):
        rows = pl.ds(c * 16, 16)
        gates = gates_ref[rows, :]
        for part in range(2):
            cols = slice(part * 256, (part + 1) * 256)
            totals = [None] * TASKS
            for e in range(EXPERTS):
                out = out_ref[e, rows, cols]
                for k in range(TASKS):
                    at = k * EXPERTS + e
                    term = out * gates[:, at : at + 1]
                    totals[k] = term if totals[k] is None else totals[k] + term
            for k in range(TASKS):
                mixed_ref[k, rows, cols] = totals[k].astype(jnp.bfloat16)
        return carry

    lax.fori_loop(0, block // 16, mix, 0)

    lane = lax.broadcasted_iota(jnp.int32, (block, LANES), 1)
    towers = []
    logit = jnp.zeros((block, LANES), jnp.float32)
    for k in range(TASKS):
        pre = jnp.dot(mixed_ref[k], tower_ref[k], preferred_element_type=jnp.float32)
        pre = pre + tower_bias_ref[k : k + 1, :]
        sigma = jax.nn.sigmoid(pre)
        out = pre * sigma
        towers.append((out, sigma + out * (1.0 - sigma)))
        score = jnp.sum(out * head_ref[k : k + 1, :], axis=1, keepdims=True)
        logit = jnp.where(lane == k, score + head_bias_ref[k], logit)
    live = live_ref[...]
    label = label_ref[...]
    softplus = jnp.maximum(logit, 0.0) + jnp.log1p(jnp.exp(-jnp.abs(logit)))
    losses = live * (softplus - label * logit)
    logit_grad = live * (jax.nn.sigmoid(logit) - label) * scale_ref[0]
    small_ref[2 * TASKS : 2 * TASKS + 1, :] += jnp.sum(logit_grad, axis=0, keepdims=True)
    small_ref[2 * TASKS + 1 : 2 * TASKS + 2, :] += jnp.sum(losses, axis=0, keepdims=True)
    for k in range(TASKS):
        out, slope = towers[k]
        signal = logit_grad[:, k : k + 1]
        small_ref[k : k + 1, 0:TOWER] += jnp.sum(signal * out, axis=0, keepdims=True)
        pre_grad = (signal * head_ref[k : k + 1, :] * slope).astype(jnp.bfloat16)
        small_ref[TASKS + k : TASKS + k + 1, 0:TOWER] += jnp.sum(
            pre_grad.astype(jnp.float32), axis=0, keepdims=True
        )
        tower_grad_ref[k] += lax.dot_general(
            mixed_ref[k], pre_grad, (((0,), (0,)), ((), ())), preferred_element_type=jnp.float32
        )
        mixed_grad_ref[k] = lax.dot_general(
            pre_grad, tower_ref[k], (((1,), (1,)), ((), ())), preferred_element_type=jnp.float32
        )

    lane8 = lax.broadcasted_iota(jnp.int32, (8, LANES), 1)

    def gate_back(c, carry):
        rows = pl.ds(c * 8, 8)
        totals = [[None] * EXPERTS for _ in range(TASKS)]
        for part in range(HID // LANES):
            cols = slice(part * LANES, (part + 1) * LANES)
            mixed = [mixed_grad_ref[k, rows, cols] for k in range(TASKS)]
            for e in range(EXPERTS):
                out = out_ref[e, rows, cols]
                for k in range(TASKS):
                    term = mixed[k] * out
                    totals[k][e] = term if totals[k][e] is None else totals[k][e] + term
        result = jnp.zeros((8, LANES), jnp.float32)
        for k in range(TASKS):
            for e in range(EXPERTS):
                value = jnp.sum(totals[k][e], axis=1, keepdims=True)
                result = jnp.where(lane8 == k * EXPERTS + e, value, result)
        gate_prob_ref[rows, :] = result
        return carry

    lax.fori_loop(0, block // 8, gate_back, 0)
    gates = gates_ref[...]
    weighed = gates * gate_prob_ref[...]
    gate_pre = weighed - gates * group_reduce(weighed, jnp.add)
    gate_grad_ref[...] = gate_pre.astype(jnp.bfloat16)

    def expert_back(c, carry):
        rows = pl.ds(c * 16, 16)
        gates = gates_ref[rows, :]
        for e in range(EXPERTS):
            column = [gates[:, k * EXPERTS + e : k * EXPERTS + e + 1] for k in range(TASKS)]
            for part in range(2):
                cols = slice(part * 256, (part + 1) * 256)
                total = None
                for k in range(TASKS):
                    term = mixed_grad_ref[k, rows, cols] * column[k]
                    total = term if total is None else total + term
                expert_grad_ref[e, rows, cols] = (total * slope_ref[e, rows, cols]).astype(
                    jnp.bfloat16
                )
        return carry

    lax.fori_loop(0, block // 16, expert_back, 0)

    transposed = (((1,), (1,)), ((), ()))
    for m in range(pairs // 2):
        low_at, high_at = m * LANES, (m + pairs // 2) * LANES
        parts = []
        for at in (low_at, high_at):
            total = lax.dot_general(
                gate_grad_ref[...],
                weight_ref[EXPERTS, at : at + LANES, 0:LANES],
                transposed,
                preferred_element_type=jnp.float32,
            )
            for e in range(EXPERTS):
                total = total + lax.dot_general(
                    expert_grad_ref[e],
                    weight_ref[e, at : at + LANES, :],
                    transposed,
                    preferred_element_type=jnp.float32,
                )
            parts.append(total)
        low, high = parts
        grad_ref[2 * m] = jnp.where(left, low, pltpu.roll(high, WIDTH, 1))
        grad_ref[2 * m + 1] = jnp.where(left, pltpu.roll(low, WIDTH, 1), high)


def dense(pooled, weights, bias, tower_bias, head, head_bias, live, label, scale, shards):
    pairs, samples = pooled.shape[:2]
    slabs, inner = weights.shape[:2]
    block = 256
    whole = lambda *shape: pl.BlockSpec(
        shape, lambda i: (0,) * len(shape), pipeline_mode=pl.Buffered(1)
    )
    kept = lambda *shape: pl.BlockSpec(shape, lambda i: (0,) * len(shape))
    smem = pl.BlockSpec(memory_space=pltpu.SMEM)
    f32, bf16 = jnp.float32, jnp.bfloat16
    return pl.pallas_call(
        functools.partial(dense_kernel, shards),
        name="dense",
        grid=(samples // block,),
        in_specs=[
            pl.BlockSpec((pairs, block, LANES), lambda i: (0, i, 0)),
            whole(slabs, inner, HID),
            whole(EXPERTS, 1, HID),
            whole(TASKS, TOWER),
            whole(TASKS, TOWER),
            smem,
            pl.BlockSpec((block, LANES), lambda i: (i, 0)),
            pl.BlockSpec((block, LANES), lambda i: (i, 0)),
            smem,
        ],
        out_specs=[
            pl.BlockSpec((pairs, block, LANES), lambda i: (0, i, 0)),
            pl.BlockSpec((EXPERTS, block, HID), lambda i: (0, i, 0)),
            pl.BlockSpec((block, inner), lambda i: (i, 0)),
            pl.BlockSpec((block, LANES), lambda i: (i, 0)),
            kept(TASKS, HID, TOWER),
            kept(16, LANES),
        ],
        out_shape=[
            jax.ShapeDtypeStruct((pairs, samples, LANES), f32),
            jax.ShapeDtypeStruct((EXPERTS, samples, HID), bf16),
            jax.ShapeDtypeStruct((samples, inner), bf16),
            jax.ShapeDtypeStruct((samples, LANES), bf16),
            jax.ShapeDtypeStruct((TASKS, HID, TOWER), f32),
            jax.ShapeDtypeStruct((16, LANES), f32),
        ],
        scratch_shapes=[
            pltpu.VMEM((block, inner), bf16),
            pltpu.VMEM((EXPERTS, block, HID), f32),
            pltpu.VMEM((EXPERTS, block, HID), f32),
            pltpu.VMEM((TASKS, block, HID), bf16),
            pltpu.VMEM((TASKS, block, HID), f32),
            pltpu.VMEM((block, LANES), f32),
            pltpu.VMEM((block, LANES), f32),
            pltpu.VMEM((TASKS, HID, TOWER), bf16),
        ],
        compiler_params=params(),
    )(pooled, weights, bias, tower_bias, head, head_bias, live, label, scale)


def weight_grad_kernel(
    shards, x_ref, expert_ref, gate_ref, tower_ref, out_ref, bias_ref, turned_ref
):
    step = pl.program_id(0)
    inner = x_ref.shape[1]
    depth = inner // shards
    half = depth // 2

    @pl.when(step == 0)
    def _():
        turned_ref[...] = x_ref[...].T

    @pl.when(step < EXPERTS)
    def _():
        grad = jnp.dot(turned_ref[...], expert_ref[0], preferred_element_type=jnp.float32)
        out_ref[0] = grad.astype(jnp.bfloat16)
        bias_ref[0] = jnp.sum(expert_ref[0].astype(jnp.float32), axis=0, keepdims=True)

    @pl.when(step == EXPERTS)
    def _():
        bias_ref[...] = jnp.zeros_like(bias_ref)
        out_ref[...] = jnp.zeros_like(out_ref)
        grad = jnp.dot(turned_ref[...], gate_ref[...], preferred_element_type=jnp.float32)
        out_ref[0, :, 0:LANES] = grad.astype(jnp.bfloat16)
        for k in range(TASKS):
            row, col = tower_spot(k, depth)
            for i in range(shards):
                out_ref[0, i * depth + row : i * depth + row + half, col : col + TOWER] = tower_ref[
                    k, i * half : (i + 1) * half, :
                ].astype(jnp.bfloat16)


def weight_grads(x, expert_grad, gate_grad, tower_grad, shards):
    samples, inner = x.shape
    whole = lambda *shape: pl.BlockSpec(
        shape, lambda i: (0,) * len(shape), pipeline_mode=pl.Buffered(1)
    )
    return pl.pallas_call(
        functools.partial(weight_grad_kernel, shards),
        name="weight_grads",
        grid=(EXPERTS + 1,),
        in_specs=[
            whole(samples, inner),
            pl.BlockSpec((1, samples, HID), lambda i: (jnp.minimum(i, EXPERTS - 1), 0, 0)),
            whole(samples, LANES),
            whole(TASKS, HID, TOWER),
        ],
        out_specs=[
            pl.BlockSpec((1, inner, HID), lambda i: (i, 0, 0)),
            pl.BlockSpec((1, 1, HID), lambda i: (i, 0, 0)),
        ],
        out_shape=[
            jax.ShapeDtypeStruct((EXPERTS + 1, inner, HID), jnp.bfloat16),
            jax.ShapeDtypeStruct((EXPERTS + 1, 1, HID), jnp.float32),
        ],
        scratch_shapes=[pltpu.VMEM((inner, samples), jnp.bfloat16)],
        compiler_params=params(),
    )(x, expert_grad, gate_grad, tower_grad)


def over_rep(value):
    if lax.axis_size("rep") == 2:
        other = lax.ppermute(value, "rep", [(0, 1), (1, 0)])
        return value.astype(jnp.float32) + other.astype(jnp.float32)
    return lax.psum(value.astype(jnp.float32), "rep")


def pack_extra(gate, tower):
    depth = gate.shape[0]
    half = depth // 2
    slab = jnp.zeros((depth, HID), gate.dtype)
    slab = lax.dynamic_update_slice(slab, gate, (0, 0))
    for k in range(TASKS):
        slab = lax.dynamic_update_slice(slab, tower[k], tower_spot(k, depth))
    return slab


def on_device(
    row_ids,
    bag_lengths,
    sample_counts,
    label_mask,
    labels,
    tables,
    table_m,
    table_v,
    expert_w,
    expert_m,
    expert_v,
    gate_w,
    gate_m,
    gate_v,
    tower_weight_matrix,
    tower_m,
    tower_v,
    small_params,
    small_m,
    small_v,
):
    shards = lax.axis_size("shard")
    device = lax.axis_index("rep") * shards + lax.axis_index("shard")
    samples, bags, longest = row_ids.shape[:3]
    rows_dev = tables.shape[0]
    depth = gate_w.shape[0]
    slots = samples * bags * longest
    capacity = slots // shards
    distinct = capacity // 4
    pairs = bags // TABLES
    int32 = jnp.int32

    own = jnp.concatenate(
        [
            expert_w.astype(jnp.bfloat16),
            pack_extra(gate_w, tower_weight_matrix).astype(jnp.bfloat16)[None],
        ],
        axis=0,
    )
    weights = lax.all_gather(own, "shard", axis=1, tiled=True)

    ids = jnp.transpose(row_ids, (1, 2, 3, 0))
    row = ids[:, :, 0, :] * ROW_BASE + ids[:, :, 1, :]
    table_of = lax.broadcasted_iota(int32, row.shape, 0) // pairs
    key = (row // rows_dev * TABLES + table_of) * rows_dev + row % rows_dev
    place = lax.broadcasted_iota(int32, row.shape, 1)
    unused = (place >= jnp.transpose(bag_lengths)[:, None, :]).astype(int32)
    number = (
        lax.broadcasted_iota(int32, row.shape, 0) * longest + place
    ) * samples + lax.broadcasted_iota(int32, row.shape, 2)
    payload = number + unused * slots
    key, payload = lax.sort(
        (key.reshape(slots), payload.reshape(slots)), num_keys=1, is_stable=False
    )
    position = jnp.arange(slots, dtype=int32)
    skipped = payload >= slots
    number = jnp.where(skipped, payload - slots, payload)
    wanted = lax.all_to_all(
        (key % rows_dev).reshape(shards, capacity), "shard", 0, 0, tiled=True
    ).reshape(slots)
    bag = number // (longest * samples)
    grad_place = jnp.where(skipped, pairs * samples, bag % pairs * samples + number % samples)
    reply_place = jnp.where(
        skipped,
        shards * distinct,
        position // capacity * distinct + position % (2 * distinct) // 2,
    )
    span = 2 * shards * distinct
    places = lax.sort(number * span + reply_place, is_stable=False) % span

    found = owner_gather(wanted, tables, shards, distinct)
    replies = lax.all_to_all(found, "shard", 0, 0, tiled=True).reshape(shards * distinct, LANES)
    pooled = pool(places, replies, samples, longest, pairs)

    first_end = EXPERTS * HID
    second_end = first_end + TASKS * TOWER
    third_end = second_end + TASKS * TOWER
    sample_total = jnp.sum(sample_counts).astype(jnp.float32)
    live_count = jnp.take(sample_counts, device)
    live = (jnp.arange(samples, dtype=int32) < live_count).astype(jnp.float32)[:, None]
    live = jnp.pad(live * label_mask.astype(jnp.float32), ((0, 0), (0, LANES - TASKS)))
    label = jnp.pad(labels.astype(jnp.float32), ((0, 0), (0, LANES - TASKS)))
    pooled_grad, expert_grad, x, gate_grad, tower_grad, sums = dense(
        pooled,
        weights,
        small_params[:first_end].reshape(EXPERTS, 1, HID),
        small_params[first_end:second_end].reshape(TASKS, TOWER),
        small_params[second_end:third_end].reshape(TASKS, TOWER),
        small_params[third_end:],
        live,
        label,
        (1.0 / sample_total).reshape(1),
        shards,
    )

    sent = grad_gather(grad_place, pooled_grad.reshape(pairs * samples, LANES), shards, distinct)
    arrived = lax.all_to_all(sent, "shard", 0, 0, tiled=True)
    table_total = over_rep(scatter(wanted, arrived, rows_dev))
    table_new, table_m_new, table_v_new = adamw(tables, table_total, table_m, table_v, rate_table)

    dense_grad, bias_grad = weight_grads(x, expert_grad, gate_grad, tower_grad, shards)
    owned = over_rep(lax.psum_scatter(dense_grad, "shard", scatter_dimension=1, tiled=True))
    extra = owned[EXPERTS]
    gate_sum = extra[:, : TASKS * EXPERTS]
    half = depth // 2
    spots = [tower_spot(k, depth) for k in range(TASKS)]
    tower_sum = jnp.stack([extra[r : r + half, c : c + TOWER] for r, c in spots])
    expert_new, expert_m_new, expert_v_new = adamw(
        expert_w, owned[:EXPERTS], expert_m, expert_v, rate_expert
    )
    gate_new, gate_m_new, gate_v_new = adamw(gate_w, gate_sum, gate_m, gate_v, rate_gate)
    tower_new, tower_m_new, tower_v_new = adamw(
        tower_weight_matrix, tower_sum, tower_m, tower_v, rate_tower
    )

    small_grad = jnp.concatenate(
        [
            bias_grad[:EXPERTS].reshape(-1),
            sums[TASKS : 2 * TASKS, :TOWER].reshape(-1),
            sums[:TASKS, :TOWER].reshape(-1),
            sums[2 * TASKS, :TASKS],
            jnp.sum(sums[2 * TASKS + 1, :TASKS]).reshape(1),
        ]
    )
    small_size = small_params.shape[0]
    padded = -(-(small_size + 1) // 1024) * 1024
    small_grad = jnp.pad(small_grad, (0, padded - small_size - 1))
    small_all = lax.all_gather(small_grad.reshape(8, padded // 8), ("rep", "shard"))
    small_sum = jnp.sum(small_all, axis=0).reshape(padded)
    small_new, small_m_new, small_v_new = adamw(
        small_params, small_sum[:small_size], small_m, small_v, rate_small
    )
    loss_parts = jnp.stack([small_sum[small_size], sample_total])
    return (
        loss_parts,
        table_new,
        table_m_new,
        table_v_new,
        expert_new,
        expert_m_new,
        expert_v_new,
        gate_new,
        gate_m_new,
        gate_v_new,
        tower_new,
        tower_m_new,
        tower_v_new,
        small_new,
        small_m_new,
        small_v_new,
    )


def solution(mesh):
    by_sample = ("rep", "shard")
    ins = (
        [P(by_sample, None, None, None), P(by_sample, None), P()]
        + [P(by_sample, None)] * 2
        + [P("shard", None)] * 3
        + [P(None, "shard", None)] * 3
        + [P("shard", None)] * 3
        + [P(None, "shard", None)] * 3
        + [P()] * 3
    )
    outs = (
        [P()]
        + [P("shard", None)] * 3
        + [P(None, "shard", None)] * 3
        + [P("shard", None)] * 3
        + [P(None, "shard", None)] * 3
        + [P()] * 3
    )
    return jax.shard_map(
        on_device, mesh=mesh, in_specs=tuple(ins), out_specs=tuple(outs), check_vma=False
    )
```

```python
import functools

import jax
import jax.numpy as jnp
from jax import lax
from jax.experimental import pallas as pl
from jax.experimental.pallas import tpu as pltpu
from jax.sharding import PartitionSpec as P

TABLES = 2
WIDTH = 64
ROW_BASE = 1024
EXPERTS = 8
HID = 512
TASKS = 5
TOWER = 64
STEP = 10
LANES = 128
UNROLL = 64
RMW = 8
PARTS = 8
PACKED = 3 * LANES
ANYWHERE = pl.BlockSpec(memory_space=pl.ANY)
VMEM_BYTES = 60 << 20

beta_first = 0.9
beta_second = 0.999
adam_epsilon = 1e-08
weight_decay = 0.01
rate_table = 1.0
rate_expert = 0.06
rate_gate = 0.03
rate_tower = 0.08
rate_small = 0.5


def adamw(weight, grad, first, second, rate):
    first_new = beta_first * first + (1.0 - beta_first) * grad
    second_new = beta_second * second + (1.0 - beta_second) * grad * grad
    first_hat = first_new / (1.0 - beta_first**STEP)
    second_hat = second_new / (1.0 - beta_second**STEP)
    weight_new = weight - rate * (
        first_hat / (jnp.sqrt(second_hat) + adam_epsilon) + weight_decay * weight
    )
    return (weight_new, first_new, second_new)


def left_lanes(rows=1):
    return lax.broadcasted_iota(jnp.int32, (rows, LANES), 1) < WIDTH


def params(**kw):
    return pltpu.CompilerParams(vmem_limit_bytes=VMEM_BYTES, **kw)


def pack(first, second, table):
    left = left_lanes(first.shape[0])
    if table == 0:
        return jnp.where(left, first, pltpu.roll(second, WIDTH, 1))
    return jnp.where(left, pltpu.roll(first, WIDTH, 1), second)


def unpack(value, table):
    turned = pltpu.roll(value, WIDTH, 1)
    return (value, turned) if table == 0 else (turned, value)


def cost(micros):
    return pl.CostEstimate(flops=0, bytes_accessed=int(micros * 1.0e2), transcendentals=0)


def owner_gather_kernel(distinct, table_at, want_ref, table_ref, out_ref, rows_ref):
    def body(step, carry):
        base = step * UNROLL
        for u in range(UNROLL):
            rows_ref[pl.ds(base + u, 1), :] = table_ref[pl.ds(want_ref[2 * (base + u)], 1), :]
        return carry

    lax.fori_loop(0, distinct // UNROLL, body, 0)
    half = distinct // 2
    packed = pack(rows_ref[0:half, :], rows_ref[half:distinct, :], table_at)
    out_ref[0] = packed.astype(jnp.bfloat16)


def owner_gather(wanted, table, shards, distinct, table_at):
    rows = table.shape[0]
    return pl.pallas_call(
        functools.partial(owner_gather_kernel, distinct, table_at),
        name="owner_gather",
        grid=(shards,),
        in_specs=[
            pl.BlockSpec((2 * distinct,), lambda i: (2 * i + table_at,), memory_space=pltpu.SMEM),
            pl.BlockSpec((rows, LANES), lambda i: (0, 0), pipeline_mode=pl.Buffered(1)),
        ],
        out_specs=pl.BlockSpec((1, distinct // 2, LANES), lambda i: (i, 0, 0)),
        out_shape=jax.ShapeDtypeStruct((shards, distinct // 2, LANES), jnp.bfloat16),
        scratch_shapes=[pltpu.VMEM((distinct, LANES), jnp.float32)],
        compiler_params=params(),
        cost_estimate=cost(20),
    )(wanted, table)


def pool_kernel(samples, longest, distinct, table_at, *refs):
    if table_at == 0:
        place_ref, reply_ref, out_ref, rows_ref, sum_ref = refs
    else:
        place_ref, reply_ref, before_ref, out_ref, rows_ref, sum_ref = refs
    shards, half = reply_ref.shape[:2]

    @pl.when(pl.program_id(0) == 0)
    def _():
        def spread(i, carry):
            first, second = unpack(reply_ref[i].astype(jnp.float32), table_at)
            base = pl.multiple_of(i * distinct, 8)
            rows_ref[pl.ds(base, half), :] = first
            rows_ref[pl.ds(base + half, half), :] = second
            return carry

        lax.fori_loop(0, shards, spread, 0)
        rows_ref[shards * distinct :, :] = jnp.zeros((8, LANES), jnp.float32)

    unroll = UNROLL // 4

    def body(step, carry):
        for u in range(unroll):
            s = step * unroll + u
            total = rows_ref[pl.ds(place_ref[s], 1), :]
            for slot in range(1, longest):
                total = total + rows_ref[pl.ds(place_ref[slot * samples + s], 1), :]
            sum_ref[pl.ds(s, 1), :] = total
        return carry

    lax.fori_loop(0, samples // unroll, body, 0)
    result = sum_ref[...]
    if table_at != 0:
        result = jnp.where(left_lanes(samples), before_ref[0].astype(jnp.float32), result)
    out_ref[0] = result.astype(jnp.bfloat16)


def pool(places, replies, before, samples, longest, pairs, table_at):
    shards, half = replies.shape[:2]
    distinct = 2 * half
    block = pl.BlockSpec((1, samples, LANES), lambda i: (i, 0, 0))
    return pl.pallas_call(
        functools.partial(pool_kernel, samples, longest, distinct, table_at),
        name="pool",
        grid=(pairs,),
        in_specs=[
            pl.BlockSpec(
                (longest * samples,), lambda i: (i + table_at * pairs,), memory_space=pltpu.SMEM
            ),
            pl.BlockSpec((shards, half, LANES), lambda i: (0, 0, 0), pipeline_mode=pl.Buffered(1)),
        ]
        + [block] * len(before),
        out_specs=block,
        out_shape=jax.ShapeDtypeStruct((pairs, samples, LANES), jnp.bfloat16),
        scratch_shapes=[
            pltpu.VMEM((shards * distinct + 8, LANES), jnp.float32),
            pltpu.VMEM((samples, LANES), jnp.float32),
        ],
        compiler_params=params(),
        cost_estimate=cost(30),
    )(places, replies, *before)


def grad_gather_kernel(distinct, table_at, index_ref, grad_ref, *refs):
    out_ref, grads_ref, rows_ref = refs[-3:]
    count = grad_ref.shape[0]

    @pl.when(pl.program_id(0) == 0)
    def _():
        grads_ref[0:count, :] = grad_ref[...]
        grads_ref[count : count + 8, :] = jnp.zeros((8, LANES), jnp.float32)

    unroll = UNROLL // 2

    def body(step, carry):
        for u in range(unroll):
            r = step * unroll + u
            first = grads_ref[pl.ds(index_ref[2 * r], 1), :]
            second = grads_ref[pl.ds(index_ref[2 * r + 1], 1), :]
            rows_ref[pl.ds(r, 1), :] = first + second
        return carry

    lax.fori_loop(0, distinct // unroll, body, 0)
    half = distinct // 2
    packed = pack(rows_ref[0:half, :], rows_ref[half:distinct, :], table_at)
    out_ref[0] = packed.astype(jnp.bfloat16)


def grad_gather(index, grads, after, shards, distinct, table_at):
    count = grads.shape[0]
    return pl.pallas_call(
        functools.partial(grad_gather_kernel, distinct, table_at),
        name="grad_gather",
        grid=(shards,),
        in_specs=[
            pl.BlockSpec((2 * distinct,), lambda i: (2 * i + table_at,), memory_space=pltpu.SMEM),
            pl.BlockSpec((count, LANES), lambda i: (0, 0), pipeline_mode=pl.Buffered(1)),
        ]
        + [ANYWHERE] * len(after),
        out_specs=pl.BlockSpec((1, distinct // 2, LANES), lambda i: (i, 0, 0)),
        out_shape=jax.ShapeDtypeStruct((shards, distinct // 2, LANES), jnp.bfloat16),
        scratch_shapes=[
            pltpu.VMEM((count + 8, LANES), jnp.float32),
            pltpu.VMEM((distinct, LANES), jnp.float32),
        ],
        compiler_params=params(),
        cost_estimate=cost(32),
    )(index, grads, *after)


def scatter_kernel(distinct, table_at, outs, want0_ref, want1_ref, got_ref, *refs):
    out_refs, (sum0_ref, sum1_ref, rows_ref) = refs[-3 - outs : -3], refs[-3:]
    half = distinct // 2
    sums = (sum0_ref, sum1_ref)
    wants = (want0_ref, want1_ref)

    @pl.when(pl.program_id(0) == 0)
    def _():
        sum0_ref[...] = jnp.zeros_like(sum0_ref)
        sum1_ref[...] = jnp.zeros_like(sum1_ref)

    for i in range(2):
        first, second = unpack(got_ref[i].astype(jnp.float32), table_at)
        rows_ref[i, 0:half, :] = first
        rows_ref[i, half:distinct, :] = second

    def put(waiting):
        ref, places, values = waiting
        for place, value in zip(places, values):
            ref[pl.ds(place, 1), :] = value

    def body(step, carry):
        waiting = None
        for part in range(PARTS):
            base = (step * PARTS + part) * RMW
            for i in range(2):
                places = [wants[i][2 * (base + u)] for u in range(RMW)]
                values = [
                    sums[i][pl.ds(places[u], 1), :] + rows_ref[i, pl.ds(base + u, 1), :]
                    for u in range(RMW)
                ]
                if waiting is not None:
                    put(waiting)
                waiting = (sums[i], places, values)
        put(waiting)
        return carry

    lax.fori_loop(0, distinct // (RMW * PARTS), body, 0)

    @pl.when(pl.program_id(0) == pl.num_programs(0) - 1)
    def _():
        count = out_refs[0].shape[0]
        chunk = count // 8
        for n, out_ref in enumerate(out_refs):

            def finish(i, carry):
                low = pl.ds(pl.multiple_of(n * count + i * chunk, 16), chunk)
                high = pl.ds(pl.multiple_of((len(out_refs) + n) * count + i * chunk, 16), chunk)
                total = pack(
                    sum0_ref[low, :] + sum1_ref[low, :],
                    sum0_ref[high, :] + sum1_ref[high, :],
                    table_at,
                )
                out_ref[pl.ds(pl.multiple_of(i * chunk, 16), chunk), :] = total.astype(jnp.bfloat16)
                return carry

            lax.fori_loop(0, 8, finish, 0)


def scatter(wanted, arrived, after, rows, table_at, outs):
    shards, half = arrived.shape[:2]
    distinct = 2 * half
    want = lambda j: pl.BlockSpec(
        (2 * distinct,), lambda i: (2 * (2 * i + j) + table_at,), memory_space=pltpu.SMEM
    )
    count = rows // 2 // outs
    return pl.pallas_call(
        functools.partial(scatter_kernel, distinct, table_at, outs),
        name="scatter",
        grid=(shards // 2,),
        in_specs=[
            want(0),
            want(1),
            pl.BlockSpec((2, half, LANES), lambda i: (i, 0, 0)),
        ]
        + [ANYWHERE] * len(after),
        out_specs=[pl.BlockSpec((count, LANES), lambda i: (0, 0))] * outs,
        out_shape=[jax.ShapeDtypeStruct((count, LANES), jnp.bfloat16)] * outs,
        scratch_shapes=[
            pltpu.VMEM((rows, LANES), jnp.float32),
            pltpu.VMEM((rows, LANES), jnp.float32),
            pltpu.VMEM((2, distinct, LANES), jnp.float32),
        ],
        compiler_params=params(),
        cost_estimate=cost(24),
    )(wanted, wanted, arrived, *after)


def table_adam_kernel(*refs):
    parts = refs[:4]
    weight_ref, first_ref, second_ref = refs[4:7]
    weight_out, first_out, second_out, token_ref = refs[-4:]
    later = pl.program_id(0) >= pl.num_programs(0) // 2
    sum0 = parts[0][...].astype(jnp.float32) + parts[1][...].astype(jnp.float32)
    sum1 = parts[2][...].astype(jnp.float32) + parts[3][...].astype(jnp.float32)
    left = left_lanes(sum0.shape[0])
    early_grad = jnp.where(left, sum0, pltpu.roll(sum1, WIDTH, 1))
    late_grad = jnp.where(left, pltpu.roll(sum0, WIDTH, 1), sum1)
    grad = jnp.where(later, late_grad, early_grad)
    weight, first, second = adamw(
        weight_ref[...], grad, first_ref[...], second_ref[...], rate_table
    )
    weight_out[...] = weight
    first_out[...] = first
    second_out[...] = second
    token_ref[...] = jnp.zeros_like(token_ref)


def table_adam(first_parts, second_parts, chunk, weight, first, second, before):
    rows = weight.shape[0]
    count = second_parts[0].shape[0]
    block = min(1024, count)
    steps = count // block
    full_at = lambda i: (chunk * steps + i % steps + i // steps * (rows // 2 // block), 0)
    inside = chunk * count % first_parts[0].shape[0] // block
    early = pl.BlockSpec((block, LANES), lambda i: (inside + i % steps, 0))
    packed = pl.BlockSpec((block, LANES), lambda i: (i % steps, 0))
    full = pl.BlockSpec((block, LANES), full_at)
    return pl.pallas_call(
        table_adam_kernel,
        name="table_adam",
        grid=(2 * steps,),
        in_specs=[early] * 2
        + [packed] * 2
        + [full] * 3
        + [pl.BlockSpec(memory_space=pl.ANY)] * len(before),
        out_specs=[full] * 3 + [pl.BlockSpec((8, LANES), lambda i: (0, 0))],
        out_shape=[jax.ShapeDtypeStruct(weight.shape, jnp.float32)] * 3
        + [jax.ShapeDtypeStruct((8, LANES), jnp.float32)],
        input_output_aliases={7 + i: i for i in range(len(before))},
        compiler_params=params(),
        cost_estimate=cost(7),
    )(*first_parts, *second_parts, weight, first, second, *before)


def group_reduce(value, op):
    lane = lax.broadcasted_iota(jnp.int32, value.shape, 1)
    shift = 1
    while shift < EXPERTS:
        other = jnp.where(
            (lane & shift) != 0,
            pltpu.roll(value, shift, 1),
            pltpu.roll(value, LANES - shift, 1),
        )
        value = op(value, other)
        shift *= 2
    return value


def dot(a, b):
    return jnp.dot(a, b, preferred_element_type=jnp.float32)


def dot_nt(a, b):
    return lax.dot_general(a, b, (((1,), (1,)), ((), ())), preferred_element_type=jnp.float32)


def dot_tn(a, b):
    return lax.dot_general(a, b, (((0,), (0,)), ((), ())), preferred_element_type=jnp.float32)


def split_two(value):
    high = value.astype(jnp.bfloat16)
    low = (value - high.astype(jnp.float32)).astype(jnp.bfloat16)
    return high, low


def dense_kernel(
    shards,
    parts,
    base_ref,
    pooled_ref,
    *refs,
):
    weight_refs, refs = refs[:parts], refs[parts:]
    dense_body(shards, base_ref, pooled_ref, weight_refs, *refs)


def dense_body(
    shards,
    base_ref,
    pooled_ref,
    weight_refs,
    bias_ref,
    tower_bias_ref,
    head_ref,
    head_bias_ref,
    live_ref,
    label_ref,
    scale_ref,
    grad_ref,
    expert_grad_ref,
    x_ref,
    gate_grad_ref,
    tower_grad_ref,
    bias_grad_ref,
    small_ref,
    out_ref,
    slope_ref,
    tower_out_ref,
    spread_ref,
    total_ref,
    tower_ref,
    expand_ref,
    head_expand_ref,
):
    pairs = pooled_ref.shape[0]
    block = pooled_ref.shape[1]
    extra_ref = weight_refs[0].at[weight_refs[0].shape[0] - 1]
    in_first = weight_refs[0].shape[0] - 1
    depth = extra_ref.shape[0] // shards
    half = depth // 2
    step = pl.program_id(0)
    f32, bf16 = jnp.float32, jnp.bfloat16

    @pl.when(step == 0)
    def _():
        for i in range(shards):
            tower_ref[i * half : (i + 1) * half, :] = extra_ref[
                i * depth : i * depth + half, LANES : LANES + PACKED
            ]
        source = lax.broadcasted_iota(jnp.int32, (LANES, PACKED), 0)
        task = lax.broadcasted_iota(jnp.int32, (LANES, PACKED), 1) // TOWER
        head_expand_ref[...] = (source == task).astype(f32).astype(bf16)
        for e in range(EXPERTS):
            expert = (base_ref[0] + e) % EXPERTS
            expand_ref[e] = (source == task * EXPERTS + expert).astype(f32).astype(bf16)
        small_ref[...] = jnp.zeros_like(small_ref)
        tower_grad_ref[...] = jnp.zeros_like(tower_grad_ref)
        bias_grad_ref[...] = jnp.zeros_like(bias_grad_ref)

    left = left_lanes(block)
    for m in range(pairs // 2):
        even = pooled_ref[2 * m].astype(f32)
        odd = pooled_ref[2 * m + 1].astype(f32)
        low = jnp.where(left, even, pltpu.roll(odd, WIDTH, 1)).astype(bf16)
        high = jnp.where(left, pltpu.roll(even, WIDTH, 1), odd).astype(bf16)
        x_ref[:, m * LANES : (m + 1) * LANES] = low
        high_at = (m + pairs // 2) * LANES
        x_ref[:, high_at : high_at + LANES] = high

    def weight(e):
        return weight_refs[0][e] if e < in_first else weight_refs[1][e - in_first]

    logits = dot(x_ref[...], extra_ref[:, 0:LANES])
    powers = jnp.exp(logits - group_reduce(logits, jnp.maximum))
    gates = powers / group_reduce(powers, jnp.add)
    gates_high, gates_low = split_two(gates)

    total_ref[...] = jnp.zeros_like(total_ref)

    def expert(e, carry):
        pre = dot(x_ref[...], weight(e)) + bias_ref[e]
        sigma = jax.nn.sigmoid(pre)
        out = pre * sigma
        slope_ref[e] = sigma + out * (1.0 - sigma)
        out_low = out.astype(bf16)
        out_ref[e] = out_low
        product = dot(out_low, tower_ref[...])
        spread = dot(gates_high, expand_ref[e]) + dot(gates_low, expand_ref[e])
        tower_out_ref[e] = product
        spread_ref[e] = spread
        total_ref[...] += spread * product
        return carry

    loop(expert)

    pre = total_ref[...] + tower_bias_ref[...]
    sigma = jax.nn.sigmoid(pre)
    tower_out = pre * sigma
    slope = sigma + tower_out * (1.0 - sigma)
    high, low = split_two(tower_out * head_ref[...])
    logit = dot_nt(high, head_expand_ref[...]) + dot_nt(low, head_expand_ref[...])
    logit = logit + head_bias_ref[...]
    live = live_ref[...]
    label = label_ref[...]
    softplus = jnp.maximum(logit, 0.0) + jnp.log1p(jnp.exp(-jnp.abs(logit)))
    losses = live * (softplus - label * logit)
    logit_grad = live * (jax.nn.sigmoid(logit) - label) * scale_ref[0]
    high, low = split_two(logit_grad)
    signal = dot(high, head_expand_ref[...]) + dot(low, head_expand_ref[...])
    pre_grad = (signal * head_ref[...] * slope).astype(bf16).astype(f32)
    small_ref[0:1, :] += jnp.sum(signal * tower_out, axis=0, keepdims=True)
    small_ref[1:2, :] += jnp.sum(pre_grad, axis=0, keepdims=True)
    small_ref[2:3, 0:LANES] += jnp.sum(logit_grad, axis=0, keepdims=True)
    small_ref[3:4, 0:LANES] += jnp.sum(losses, axis=0, keepdims=True)

    total_ref[...] = pre_grad

    def back(e, carry):
        gate_prob, pooled_grad = carry
        pre_grad = total_ref[...]
        weighed = (spread_ref[e] * pre_grad).astype(bf16)
        tower_grad_ref[...] += dot_tn(weighed, out_ref[e])
        expert_grad = (dot_nt(weighed, tower_ref[...]) * slope_ref[e]).astype(bf16)
        expert_grad_ref[e] = expert_grad
        bias_grad_ref[e] += jnp.sum(expert_grad.astype(f32), axis=0, keepdims=True)
        high, low = split_two(tower_out_ref[e] * pre_grad)
        gate_prob = gate_prob + dot_nt(high, expand_ref[e]) + dot_nt(low, expand_ref[e])
        pooled_grad = pooled_grad + dot_nt(expert_grad, weight(e))
        return gate_prob, pooled_grad

    gate_prob, pooled_grad = loop(
        back, (jnp.zeros((block, LANES), f32), jnp.zeros((block, pairs * LANES), f32))
    )
    weighed = gates * gate_prob
    gate_grad = (weighed - gates * group_reduce(weighed, jnp.add)).astype(bf16)
    gate_grad_ref[...] = gate_grad
    pooled_grad = pooled_grad + dot_nt(gate_grad, extra_ref[:, 0:LANES])
    for m in range(pairs // 2):
        low = pooled_grad[:, m * LANES : (m + 1) * LANES]
        high_at = (m + pairs // 2) * LANES
        high = pooled_grad[:, high_at : high_at + LANES]
        grad_ref[2 * m] = jnp.where(left, low, pltpu.roll(high, WIDTH, 1))
        grad_ref[2 * m + 1] = jnp.where(left, pltpu.roll(low, WIDTH, 1), high)


def loop(body, carry=0):
    for e in range(EXPERTS):
        carry = body(e, carry)
    return carry


def dense(base, pooled, weights, bias, tower_bias, head, head_bias, live, label, scale, shards):
    pairs, samples = pooled.shape[:2]
    inner = weights[0].shape[1]
    slabs = [weights[0].shape[0], EXPERTS + 1 - weights[0].shape[0]][: len(weights)]
    block = 256
    whole = lambda *shape: pl.BlockSpec(
        shape, lambda i: (0,) * len(shape), pipeline_mode=pl.Buffered(1)
    )
    kept = lambda *shape: pl.BlockSpec(shape, lambda i: (0,) * len(shape))
    f32, bf16 = jnp.float32, jnp.bfloat16
    return pl.pallas_call(
        functools.partial(dense_kernel, shards, len(weights)),
        name="dense",
        grid=(samples // block,),
        in_specs=[
            pl.BlockSpec(memory_space=pltpu.SMEM),
            pl.BlockSpec((pairs, block, LANES), lambda i: (0, i, 0)),
        ]
        + [whole(n, inner, HID) for n in slabs]
        + [
            whole(EXPERTS, 1, HID),
            whole(1, PACKED),
            whole(1, PACKED),
            whole(1, LANES),
            pl.BlockSpec((block, LANES), lambda i: (i, 0)),
            pl.BlockSpec((block, LANES), lambda i: (i, 0)),
            pl.BlockSpec(memory_space=pltpu.SMEM),
        ],
        out_specs=[
            pl.BlockSpec((pairs, block, LANES), lambda i: (0, i, 0)),
            pl.BlockSpec((EXPERTS, block, HID), lambda i: (0, i, 0)),
            pl.BlockSpec((block, inner), lambda i: (i, 0)),
            pl.BlockSpec((block, LANES), lambda i: (i, 0)),
            kept(PACKED, HID),
            kept(EXPERTS, 1, HID),
            kept(8, PACKED),
        ],
        out_shape=[
            jax.ShapeDtypeStruct((pairs, samples, LANES), f32),
            jax.ShapeDtypeStruct((EXPERTS, samples, HID), bf16),
            jax.ShapeDtypeStruct((samples, inner), bf16),
            jax.ShapeDtypeStruct((samples, LANES), bf16),
            jax.ShapeDtypeStruct((PACKED, HID), f32),
            jax.ShapeDtypeStruct((EXPERTS, 1, HID), f32),
            jax.ShapeDtypeStruct((8, PACKED), f32),
        ],
        scratch_shapes=[
            pltpu.VMEM((EXPERTS, block, HID), bf16),
            pltpu.VMEM((EXPERTS, block, HID), f32),
            pltpu.VMEM((EXPERTS, block, PACKED), f32),
            pltpu.VMEM((EXPERTS, block, PACKED), f32),
            pltpu.VMEM((block, PACKED), f32),
            pltpu.VMEM((HID, PACKED), bf16),
            pltpu.VMEM((EXPERTS, LANES, PACKED), bf16),
            pltpu.VMEM((LANES, PACKED), bf16),
        ],
        compiler_params=params(),
        cost_estimate=cost(60),
    )(base, pooled, *weights, bias, tower_bias, head, head_bias, live, label, scale)


def weight_grad_kernel(
    shards, which_ref, x_ref, expert_ref, gate_ref, tower_ref, out_ref, extra_ref, turned_ref
):
    step = pl.program_id(0)
    last = pl.num_programs(0) - 1
    inner = x_ref.shape[1]
    depth = inner // shards
    half = depth // 2

    @pl.when(step == 0)
    def _():
        turned_ref[...] = x_ref[...].T

    @pl.when(step < last)
    def _():
        out_ref[0] = dot(turned_ref[...], expert_ref[0]).astype(jnp.bfloat16)

    @pl.when(step == last)
    def _():
        gate = dot(turned_ref[...], gate_ref[...])
        extra_ref[0, :, 0:LANES] = gate.astype(jnp.bfloat16)
        turned = tower_ref[...].T
        none = jnp.zeros((depth - half, PACKED), jnp.float32)
        runs = []
        for i in range(shards):
            runs += [turned[i * half : (i + 1) * half, :], none]
        extra_ref[0, :, LANES:] = jnp.concatenate(runs, axis=0).astype(jnp.bfloat16)


def weight_grads(which, x, expert_grad, gate_grad, tower_grad, shards):
    samples, inner = x.shape
    count = which.shape[0]
    whole = lambda *shape: pl.BlockSpec(
        shape, lambda i, w: (0,) * len(shape), pipeline_mode=pl.Buffered(1)
    )
    upto = lambda i: jnp.minimum(i, count - 1)
    return pl.pallas_call(
        functools.partial(weight_grad_kernel, shards),
        name="weight_grads",
        grid_spec=pltpu.PrefetchScalarGridSpec(
            num_scalar_prefetch=1,
            grid=(count + 1,),
            in_specs=[
                whole(samples, inner),
                pl.BlockSpec((1, samples, HID), lambda i, w: (w[upto(i)], 0, 0)),
                whole(samples, LANES),
                whole(PACKED, HID),
            ],
            out_specs=[
                pl.BlockSpec((1, inner, HID), lambda i, w: (upto(i), 0, 0)),
                pl.BlockSpec((1, inner, HID), lambda i, w: (0, 0, 0)),
            ],
            scratch_shapes=[pltpu.VMEM((inner, samples), jnp.bfloat16)],
        ),
        out_shape=[
            jax.ShapeDtypeStruct((count, inner, HID), jnp.bfloat16),
            jax.ShapeDtypeStruct((1, inner, HID), jnp.bfloat16),
        ],
        compiler_params=params(),
        cost_estimate=cost(18),
    )(which, x, expert_grad, gate_grad, tower_grad)


def order(value, *after):
    return pl.pallas_call(
        lambda *refs: None,
        name="order",
        in_specs=[ANYWHERE] * (1 + len(after)),
        out_specs=ANYWHERE,
        out_shape=jax.ShapeDtypeStruct(value.shape, value.dtype),
        input_output_aliases={0: 0},
    )(value, *after)


def dense_adam_kernel(part, rep_ref, here_ref, there_ref, more_ref, other_ref, *refs):
    expert, gate, tower = refs[0:3], refs[3:6], refs[6:9]
    expert_out, gate_out, tower_out = refs[9:12], refs[12:15], refs[15:18]
    step = pl.program_id(0)
    depth = more_ref.shape[1]
    half = depth // 2

    def put(outs, at, values):
        for out_ref, value in zip(outs, values):
            out_ref[at] = value

    grad = there_ref[0].astype(jnp.float32)
    if part < EXPERTS:
        mine = rep_ref[0] == step // part
        grad = jnp.where(mine, here_ref[0].astype(jnp.float32), grad)
    put(expert_out, 0, adamw(expert[0][0], grad, expert[1][0], expert[2][0], rate_expert))

    @pl.when(step == 0)
    def _():
        grad = more_ref[0].astype(jnp.float32) + other_ref[0].astype(jnp.float32)
        gate_grad = grad[:, 0:LANES].T[0 : TASKS * EXPERTS, :]
        put(gate_out, ..., adamw(gate[0][...], gate_grad, gate[1][...], gate[2][...], rate_gate))
        for k in range(TASKS):
            tower_grad = grad[0:half, LANES + k * TOWER : LANES + (k + 1) * TOWER]
            put(tower_out, k, adamw(tower[0][k], tower_grad, tower[1][k], tower[2][k], rate_tower))


def dense_adam(rep, here, there, extra, expert, gate, tower):
    part = here.shape[0]
    count, depth = expert[0].shape[:2]
    slab = lambda at: pl.BlockSpec((1, depth, HID), lambda i: (at(i), 0, 0))
    whole = lambda value: pl.BlockSpec(value.shape, lambda i: (0,) * value.ndim)
    arrays = [*expert, *gate, *tower]
    specs = [slab(lambda i: i)] * 3 + [whole(value) for value in arrays[3:]]
    outs = pl.pallas_call(
        functools.partial(dense_adam_kernel, part),
        name="dense_adam",
        grid=(count,),
        in_specs=[
            pl.BlockSpec(memory_space=pltpu.SMEM),
            slab(lambda i: i % part),
            slab(lambda i: i % part),
            slab(lambda i: extra[0].shape[0] - 1),
            slab(lambda i: extra[1].shape[0] - 1),
        ]
        + specs,
        out_specs=specs,
        out_shape=[jax.ShapeDtypeStruct(value.shape, jnp.float32) for value in arrays],
        compiler_params=params(),
    )(rep, here, there, *extra, *arrays)
    return outs[0:3], outs[3:6], outs[6:9]


def swap_rep(value):
    return lax.ppermute(value, "rep", [(0, 1), (1, 0)])


def sum_everywhere(value):
    for axis in ("shard", "rep"):
        size = lax.axis_size(axis)
        if size & (size - 1):
            value = lax.psum(value, axis)
            continue
        shift = 1
        while shift < size:
            value = value + lax.ppermute(value, axis, [(i, i ^ shift) for i in range(size)])
            shift *= 2
    return value


def pack_extra(gate, tower):
    depth = gate.shape[0]
    half = depth // 2
    side = jnp.transpose(tower, (1, 0, 2)).reshape(half, TASKS * TOWER)
    slab = jnp.pad(gate, ((0, 0), (0, HID - gate.shape[1])))
    return slab + jnp.pad(side, ((0, depth - half), (LANES, HID - LANES - TASKS * TOWER)))


def on_device(
    row_ids,
    bag_lengths,
    sample_counts,
    label_mask,
    labels,
    tables,
    table_m,
    table_v,
    expert_w,
    expert_m,
    expert_v,
    gate_w,
    gate_m,
    gate_v,
    tower_weight_matrix,
    tower_m,
    tower_v,
    small_params,
    small_m,
    small_v,
):
    shards = lax.axis_size("shard")
    reps = lax.axis_size("rep")
    rep = lax.axis_index("rep")
    device = rep * shards + lax.axis_index("shard")
    samples, bags, longest = row_ids.shape[:3]
    rows_dev = tables.shape[0]
    depth = gate_w.shape[0]
    half = depth // 2
    slots = samples * bags * longest
    capacity = slots // shards
    distinct = capacity // 4
    pairs = bags // TABLES
    int32 = jnp.int32
    both = range(TABLES)

    extra = pack_extra(gate_w, tower_weight_matrix)[None]
    if reps == 2:
        part = EXPERTS // 2
        base = rep * part
        line = jnp.arange(part, dtype=int32)
        chosen = jnp.where(rep == 0, expert_w[:part], expert_w[part:])
    else:
        base = jnp.zeros_like(rep)
        chosen = expert_w
    own = jnp.concatenate([chosen, extra], axis=0).astype(jnp.bfloat16)
    weights = [lax.all_gather(own, "shard", axis=1, tiled=True)]
    if reps == 2:
        weights += [swap_rep(weights[0][:part])]

    def by_slot(value):
        if reps != 2:
            return value
        turned = jnp.concatenate([value[part:], value[:part]], axis=0)
        return jnp.where(rep == 0, value, turned)

    ids = jnp.transpose(row_ids, (1, 2, 3, 0))
    row = ids[:, :, 0, :] * ROW_BASE + ids[:, :, 1, :]
    table_of = lax.broadcasted_iota(int32, row.shape, 0) // pairs
    key = (row // rows_dev * TABLES + table_of) * rows_dev + row % rows_dev
    place = lax.broadcasted_iota(int32, row.shape, 1)
    unused = (place >= jnp.transpose(bag_lengths)[:, None, :]).astype(int32)
    number = (
        lax.broadcasted_iota(int32, row.shape, 0) * longest + place
    ) * samples + lax.broadcasted_iota(int32, row.shape, 2)
    payload = number + unused * slots
    key, payload = lax.sort(
        (key.reshape(slots), payload.reshape(slots)), num_keys=1, is_stable=False
    )
    position = jnp.arange(slots, dtype=int32)
    skipped = payload >= slots
    number = jnp.where(skipped, payload - slots, payload)
    wanted = lax.all_to_all(
        (key % rows_dev).reshape(shards, capacity), "shard", 0, 0, tiled=True
    ).reshape(slots)
    bag = number // (longest * samples)
    grad_place = jnp.where(skipped, pairs * samples, bag % pairs * samples + number % samples)
    reply_place = jnp.where(
        skipped,
        shards * distinct,
        position // capacity * distinct + position % (2 * distinct) // 2,
    )
    span = 2 * shards * distinct
    places = lax.sort(number * span + reply_place, is_stable=False) % span

    def exchange(value):
        return lax.all_to_all(value, "shard", 0, 0, tiled=True)

    found = [owner_gather(wanted, tables, shards, distinct, t) for t in both]
    found[1], places = lax.optimization_barrier((found[1], places))
    replies = [exchange(value) for value in found]
    pooled = []
    for t in both:
        pooled = [pool(places, replies[t], pooled, samples, longest, pairs, t)]

    first_end = EXPERTS * HID
    second_end = first_end + TASKS * TOWER
    third_end = second_end + TASKS * TOWER
    fill = PACKED - TASKS * TOWER
    sample_total = jnp.sum(sample_counts).astype(jnp.float32)
    live_count = jnp.take(sample_counts, device)
    live = (jnp.arange(samples, dtype=int32) < live_count).astype(jnp.float32)[:, None]
    live = jnp.pad(live * label_mask.astype(jnp.float32), ((0, 0), (0, LANES - TASKS)))
    label = jnp.pad(labels.astype(jnp.float32), ((0, 0), (0, LANES - TASKS)))
    pooled_grad, expert_grad, x, gate_grad, tower_grad, bias_grad, sums = dense(
        base.astype(int32).reshape(1),
        pooled[0],
        weights,
        by_slot(small_params[:first_end].reshape(EXPERTS, 1, HID)),
        jnp.pad(small_params[first_end:second_end], (0, fill)).reshape(1, PACKED),
        jnp.pad(small_params[second_end:third_end], (0, fill)).reshape(1, PACKED),
        jnp.pad(small_params[third_end:], (0, LANES - TASKS)).reshape(1, LANES),
        live,
        label,
        (1.0 / sample_total).reshape(1),
        shards,
    )

    every = jnp.arange(EXPERTS, dtype=int32)
    kept, extra_grad = weight_grads(
        (every - base.astype(int32)) % EXPERTS, x, expert_grad, gate_grad, tower_grad, shards
    )
    if reps == 2:
        kept = lax.psum_scatter(kept, "rep", scatter_dimension=0, tiled=True)

    def owned_sum(value):
        return lax.psum_scatter(value, "shard", scatter_dimension=1, tiled=True)

    small_grad = jnp.concatenate(
        [
            by_slot(bias_grad).reshape(-1),
            sums[1, : TASKS * TOWER],
            sums[0, : TASKS * TOWER],
            sums[2, :TASKS],
            jnp.sum(sums[3, :TASKS]).reshape(1),
        ]
    )
    small_size = small_params.shape[0]
    padded = -(-(small_size + 1) // 1024) * 1024
    small_grad = jnp.pad(small_grad, (0, padded - small_size - 1))
    small_grad = small_grad.reshape(padded // LANES, LANES)
    pooled_grad = pooled_grad.reshape(pairs * samples, LANES)
    sent = []
    for t in both:
        sent.append(grad_gather(grad_place, pooled_grad, sent[:], shards, distinct, t))
    arrived = [exchange(value) for value in sent]
    chunks = (2, 2)
    table_parts = []
    after = [sent[1]]
    for t in both:
        mine = scatter(wanted, arrived[t], after, rows_dev, t, chunks[t])
        if reps == 2:
            table_parts.append([])
            for n, value in enumerate(mine):
                if t == 1:
                    value = order(value, (table_parts[0] + table_parts[1])[-1][1])
                table_parts[t].append((value, swap_rep(value)))
            after = [table_parts[0][0][1]]
        else:
            table_parts.append(
                [(lax.psum(v.astype(jnp.float32), "rep"), jnp.zeros_like(v)) for v in mine]
            )

    table_state = []
    tokens = []
    for chunk, second_parts in enumerate(table_parts[1]):
        first_parts = table_parts[0][chunk * chunks[0] // chunks[1]]
        *table_state, token = table_adam(
            first_parts, second_parts, chunk, tables, table_m, table_v, table_state
        )
        tokens.append(token)
    table_new, table_m_new, table_v_new = table_state

    kept = jnp.concatenate([kept, extra_grad], axis=0)
    if reps == 2:
        kept = order(kept, arrived[1], table_parts[0][0][1])
    summed = owned_sum(kept)
    expert = (expert_w, expert_m, expert_v)
    gate = [jnp.transpose(value) for value in (gate_w, gate_m, gate_v)]
    tower = (tower_weight_matrix, tower_m, tower_v)
    if reps == 2:
        summed = order(summed, tokens[-1])
        small_grad = order(small_grad, summed)
        there = swap_rep(summed)
        here = summed[:part]
        extra = (summed, there)
    else:
        here = lax.psum(summed.astype(jnp.float32), "rep")
        there = here
        extra = (here, jnp.zeros_like(here))
        here = here[:EXPERTS]
    expert_new, gate_new, tower_new = dense_adam(
        rep.astype(int32).reshape(1), here, there, extra, expert, gate, tower
    )
    expert_new, expert_m_new, expert_v_new = expert_new
    gate_new, gate_m_new, gate_v_new = [jnp.transpose(value) for value in gate_new]
    tower_new, tower_m_new, tower_v_new = tower_new
    small_sum = sum_everywhere(small_grad).reshape(padded)
    small_new, small_m_new, small_v_new = adamw(
        small_params, small_sum[:small_size], small_m, small_v, rate_small
    )
    loss_parts = jnp.stack([small_sum[small_size], sample_total])
    return (
        loss_parts,
        table_new,
        table_m_new,
        table_v_new,
        expert_new,
        expert_m_new,
        expert_v_new,
        gate_new,
        gate_m_new,
        gate_v_new,
        tower_new,
        tower_m_new,
        tower_v_new,
        small_new,
        small_m_new,
        small_v_new,
    )


def solution(mesh):
    by_sample = ("rep", "shard")
    ins = (
        [P(by_sample, None, None, None), P(by_sample, None), P()]
        + [P(by_sample, None)] * 2
        + [P("shard", None)] * 3
        + [P(None, "shard", None)] * 3
        + [P("shard", None)] * 3
        + [P(None, "shard", None)] * 3
        + [P()] * 3
    )
    outs = (
        [P()]
        + [P("shard", None)] * 3
        + [P(None, "shard", None)] * 3
        + [P("shard", None)] * 3
        + [P(None, "shard", None)] * 3
        + [P()] * 3
    )
    return jax.shard_map(
        on_device, mesh=mesh, in_specs=tuple(ins), out_specs=tuple(outs), check_vma=False
    )
```

```python
import functools

import jax
import jax.numpy as jnp
from jax import lax
from jax.experimental import pallas as pl
from jax.experimental.pallas import tpu as pltpu
from jax.sharding import PartitionSpec as P

TABLES = 2
WIDTH = 64
ROW_BASE = 1024
EXPERTS = 8
HID = 512
TASKS = 5
TOWER = 64
STEP = 10
LANES = 128
UNROLL = 256
RMW = 8
PARTS = 8
PACKED = 3 * LANES
ANYWHERE = pl.BlockSpec(memory_space=pl.ANY)
VMEM_BYTES = 60 << 20

beta_first = 0.9
beta_second = 0.999
adam_epsilon = 1e-08
weight_decay = 0.01
rate_table = 1.0
rate_expert = 0.06
rate_gate = 0.03
rate_tower = 0.08
rate_small = 0.5


def adamw(weight, grad, first, second, rate):
    first_new = beta_first * first + (1.0 - beta_first) * grad
    second_new = beta_second * second + (1.0 - beta_second) * grad * grad
    first_hat = first_new / (1.0 - beta_first**STEP)
    second_hat = second_new / (1.0 - beta_second**STEP)
    weight_new = weight - rate * (
        first_hat / (jnp.sqrt(second_hat) + adam_epsilon) + weight_decay * weight
    )
    return (weight_new, first_new, second_new)


def left_lanes(rows=1):
    return lax.broadcasted_iota(jnp.int32, (rows, LANES), 1) < WIDTH


def params(**kw):
    return pltpu.CompilerParams(vmem_limit_bytes=VMEM_BYTES, **kw)


def pack(first, second, table):
    left = left_lanes(first.shape[0])
    if table == 0:
        return jnp.where(left, first, pltpu.roll(second, WIDTH, 1))
    return jnp.where(left, pltpu.roll(first, WIDTH, 1), second)


def unpack(value, table):
    turned = pltpu.roll(value, WIDTH, 1)
    return (value, turned) if table == 0 else (turned, value)


def cost(micros):
    return pl.CostEstimate(flops=0, bytes_accessed=int(micros * 1.0e2), transcendentals=0)


def owner_gather_kernel(distinct, table_at, want_ref, table_ref, *refs):
    out_ref, rows_ref = refs[-2:]

    def body(step, carry):
        base = step * UNROLL
        for u in range(UNROLL):
            rows_ref[pl.ds(base + u, 1), :] = table_ref[pl.ds(want_ref[2 * (base + u)], 1), :]
        return carry

    lax.fori_loop(0, distinct // UNROLL, body, 0)
    half = distinct // 2
    packed = pack(rows_ref[0:half, :], rows_ref[half:distinct, :], table_at)
    out_ref[0] = packed.astype(jnp.bfloat16)


def owner_gather(wanted, table, after, shards, distinct, table_at):
    rows = table.shape[0]
    return pl.pallas_call(
        functools.partial(owner_gather_kernel, distinct, table_at),
        name="owner_gather",
        grid=(shards,),
        in_specs=[
            pl.BlockSpec((2 * distinct,), lambda i: (i,), memory_space=pltpu.SMEM),
            pl.BlockSpec((rows, LANES), lambda i: (0, 0), pipeline_mode=pl.Buffered(1)),
        ]
        + [ANYWHERE] * len(after),
        out_specs=pl.BlockSpec((1, distinct // 2, LANES), lambda i: (i, 0, 0)),
        out_shape=jax.ShapeDtypeStruct((shards, distinct // 2, LANES), jnp.bfloat16),
        scratch_shapes=[pltpu.VMEM((distinct, LANES), jnp.float32)],
        compiler_params=params(),
        cost_estimate=cost(20),
    )(wanted, table, *after)


def pool_kernel(samples, longest, distinct, table_at, *refs):
    if table_at == 0:
        place_ref, reply_ref, out_ref, rows_ref, sum_ref = refs
    else:
        place_ref, reply_ref, before_ref, out_ref, rows_ref, sum_ref = refs
    shards, half = reply_ref.shape[:2]

    @pl.when(pl.program_id(0) == 0)
    def _():
        def spread(i, carry):
            first, second = unpack(reply_ref[i].astype(jnp.float32), table_at)
            base = pl.multiple_of(i * distinct, 8)
            rows_ref[pl.ds(base, half), :] = first
            rows_ref[pl.ds(base + half, half), :] = second
            return carry

        lax.fori_loop(0, shards, spread, 0)
        rows_ref[shards * distinct :, :] = jnp.zeros((8, LANES), jnp.float32)

    unroll = UNROLL // 4

    def body(step, carry):
        for u in range(unroll):
            s = step * unroll + u
            total = rows_ref[pl.ds(place_ref[s], 1), :]
            for slot in range(1, longest):
                total = total + rows_ref[pl.ds(place_ref[slot * samples + s], 1), :]
            sum_ref[pl.ds(s, 1), :] = total
        return carry

    lax.fori_loop(0, samples // unroll, body, 0)
    result = sum_ref[...]
    if table_at != 0:
        result = jnp.where(left_lanes(samples), before_ref[0].astype(jnp.float32), result)
    out_ref[0] = result.astype(jnp.bfloat16)


def pool(places, replies, before, samples, longest, pairs, table_at):
    shards, half = replies.shape[:2]
    distinct = 2 * half
    block = pl.BlockSpec((1, samples, LANES), lambda i: (i, 0, 0))
    return pl.pallas_call(
        functools.partial(pool_kernel, samples, longest, distinct, table_at),
        name="pool",
        grid=(pairs,),
        in_specs=[
            pl.BlockSpec(
                (longest * samples,), lambda i: (i,), memory_space=pltpu.SMEM
            ),
            pl.BlockSpec((shards, half, LANES), lambda i: (0, 0, 0), pipeline_mode=pl.Buffered(1)),
        ]
        + [block] * len(before),
        out_specs=block,
        out_shape=jax.ShapeDtypeStruct((pairs, samples, LANES), jnp.bfloat16),
        scratch_shapes=[
            pltpu.VMEM((shards * distinct + 8, LANES), jnp.float32),
            pltpu.VMEM((samples, LANES), jnp.float32),
        ],
        compiler_params=params(),
        cost_estimate=cost(30),
    )(places, replies, *before)


def grad_gather_kernel(distinct, table_at, index_ref, grad_ref, *refs):
    out_ref, grads_ref, rows_ref = refs[-3:]
    count = grad_ref.shape[0]

    @pl.when(pl.program_id(0) == 0)
    def _():
        grads_ref[0:count, :] = grad_ref[...]
        grads_ref[count : count + 8, :] = jnp.zeros((8, LANES), jnp.float32)

    unroll = UNROLL // 2

    def body(step, carry):
        for u in range(unroll):
            r = step * unroll + u
            first = grads_ref[pl.ds(index_ref[2 * r], 1), :]
            second = grads_ref[pl.ds(index_ref[2 * r + 1], 1), :]
            rows_ref[pl.ds(r, 1), :] = first + second
        return carry

    lax.fori_loop(0, distinct // unroll, body, 0)
    half = distinct // 2
    packed = pack(rows_ref[0:half, :], rows_ref[half:distinct, :], table_at)
    out_ref[0] = packed.astype(jnp.bfloat16)


def grad_gather(index, grads, after, shards, distinct, table_at):
    count = grads.shape[0]
    return pl.pallas_call(
        functools.partial(grad_gather_kernel, distinct, table_at),
        name="grad_gather",
        grid=(shards,),
        in_specs=[
            pl.BlockSpec((2 * distinct,), lambda i: (i,), memory_space=pltpu.SMEM),
            pl.BlockSpec((count, LANES), lambda i: (0, 0), pipeline_mode=pl.Buffered(1)),
        ]
        + [ANYWHERE] * len(after),
        out_specs=pl.BlockSpec((1, distinct // 2, LANES), lambda i: (i, 0, 0)),
        out_shape=jax.ShapeDtypeStruct((shards, distinct // 2, LANES), jnp.bfloat16),
        scratch_shapes=[
            pltpu.VMEM((count + 8, LANES), jnp.float32),
            pltpu.VMEM((distinct, LANES), jnp.float32),
        ],
        compiler_params=params(),
        cost_estimate=cost(32),
    )(index, grads, *after)


def scatter_kernel(distinct, table_at, outs, want0_ref, want1_ref, got_ref, *refs):
    out_refs, (sum0_ref, sum1_ref, rows_ref) = refs[-3 - outs : -3], refs[-3:]
    half = distinct // 2
    sums = (sum0_ref, sum1_ref)
    wants = (want0_ref, want1_ref)

    @pl.when(pl.program_id(0) == 0)
    def _():
        sum0_ref[...] = jnp.zeros_like(sum0_ref)
        sum1_ref[...] = jnp.zeros_like(sum1_ref)

    for i in range(2):
        first, second = unpack(got_ref[i].astype(jnp.float32), table_at)
        rows_ref[i, 0:half, :] = first
        rows_ref[i, half:distinct, :] = second

    def put(waiting):
        ref, places, values = waiting
        for place, value in zip(places, values):
            ref[pl.ds(place, 1), :] = value

    def body(step, carry):
        waiting = None
        for part in range(PARTS):
            base = (step * PARTS + part) * RMW
            for i in range(2):
                places = [wants[i][2 * (base + u)] for u in range(RMW)]
                values = [
                    sums[i][pl.ds(places[u], 1), :] + rows_ref[i, pl.ds(base + u, 1), :]
                    for u in range(RMW)
                ]
                if waiting is not None:
                    put(waiting)
                waiting = (sums[i], places, values)
        put(waiting)
        return carry

    lax.fori_loop(0, distinct // (RMW * PARTS), body, 0)

    @pl.when(pl.program_id(0) == pl.num_programs(0) - 1)
    def _():
        count = out_refs[0].shape[0]
        chunk = count // 8
        for n, out_ref in enumerate(out_refs):

            def finish(i, carry):
                low = pl.ds(pl.multiple_of(n * count + i * chunk, 16), chunk)
                high = pl.ds(pl.multiple_of((len(out_refs) + n) * count + i * chunk, 16), chunk)
                total = pack(
                    sum0_ref[low, :] + sum1_ref[low, :],
                    sum0_ref[high, :] + sum1_ref[high, :],
                    table_at,
                )
                out_ref[pl.ds(pl.multiple_of(i * chunk, 16), chunk), :] = total.astype(jnp.bfloat16)
                return carry

            lax.fori_loop(0, 8, finish, 0)


def scatter(wanted, arrived, after, rows, table_at, outs):
    shards, half = arrived.shape[:2]
    distinct = 2 * half
    want = lambda j: pl.BlockSpec(
        (2 * distinct,), lambda i: (2 * i + j,), memory_space=pltpu.SMEM
    )
    count = rows // 2 // outs
    return pl.pallas_call(
        functools.partial(scatter_kernel, distinct, table_at, outs),
        name="scatter",
        grid=(shards // 2,),
        in_specs=[
            want(0),
            want(1),
            pl.BlockSpec((2, half, LANES), lambda i: (i, 0, 0)),
        ]
        + [ANYWHERE] * len(after),
        out_specs=[pl.BlockSpec((count, LANES), lambda i: (0, 0))] * outs,
        out_shape=[jax.ShapeDtypeStruct((count, LANES), jnp.bfloat16)] * outs,
        scratch_shapes=[
            pltpu.VMEM((rows, LANES), jnp.float32),
            pltpu.VMEM((rows, LANES), jnp.float32),
            pltpu.VMEM((2, distinct, LANES), jnp.float32),
        ],
        compiler_params=params(),
        cost_estimate=cost(24),
    )(wanted, wanted, arrived, *after)


def table_adam_kernel(*refs):
    parts = refs[:4]
    weight_ref, first_ref, second_ref = refs[4:7]
    weight_out, first_out, second_out, token_ref = refs[-4:]
    later = pl.program_id(0) >= pl.num_programs(0) // 2
    sum0 = parts[0][...].astype(jnp.float32) + parts[1][...].astype(jnp.float32)
    sum1 = parts[2][...].astype(jnp.float32) + parts[3][...].astype(jnp.float32)
    left = left_lanes(sum0.shape[0])
    early_grad = jnp.where(left, sum0, pltpu.roll(sum1, WIDTH, 1))
    late_grad = jnp.where(left, pltpu.roll(sum0, WIDTH, 1), sum1)
    grad = jnp.where(later, late_grad, early_grad)
    weight, first, second = adamw(
        weight_ref[...], grad, first_ref[...], second_ref[...], rate_table
    )
    weight_out[...] = weight
    first_out[...] = first
    second_out[...] = second
    token_ref[...] = jnp.zeros_like(token_ref)


def table_adam(first_parts, second_parts, chunk, weight, first, second, before):
    rows = weight.shape[0]
    count = second_parts[0].shape[0]
    block = min(1024, count)
    steps = count // block
    full_at = lambda i: (chunk * steps + i % steps + i // steps * (rows // 2 // block), 0)
    inside = chunk * count % first_parts[0].shape[0] // block
    early = pl.BlockSpec((block, LANES), lambda i: (inside + i % steps, 0))
    packed = pl.BlockSpec((block, LANES), lambda i: (i % steps, 0))
    full = pl.BlockSpec((block, LANES), full_at)
    return pl.pallas_call(
        table_adam_kernel,
        name="table_adam",
        grid=(2 * steps,),
        in_specs=[early] * 2
        + [packed] * 2
        + [full] * 3
        + [pl.BlockSpec(memory_space=pl.ANY)] * len(before),
        out_specs=[full] * 3 + [pl.BlockSpec((8, LANES), lambda i: (0, 0))],
        out_shape=[jax.ShapeDtypeStruct(weight.shape, jnp.float32)] * 3
        + [jax.ShapeDtypeStruct((8, LANES), jnp.float32)],
        input_output_aliases={7 + i: i for i in range(len(before))},
        compiler_params=params(),
        cost_estimate=cost(7),
    )(*first_parts, *second_parts, weight, first, second, *before)


def group_reduce(value, op):
    lane = lax.broadcasted_iota(jnp.int32, value.shape, 1)
    shift = 1
    while shift < EXPERTS:
        other = jnp.where(
            (lane & shift) != 0,
            pltpu.roll(value, shift, 1),
            pltpu.roll(value, LANES - shift, 1),
        )
        value = op(value, other)
        shift *= 2
    return value


def dot(a, b):
    return jnp.dot(a, b, preferred_element_type=jnp.float32)


def dot_nt(a, b):
    return lax.dot_general(a, b, (((1,), (1,)), ((), ())), preferred_element_type=jnp.float32)


def dot_tn(a, b):
    return lax.dot_general(a, b, (((0,), (0,)), ((), ())), preferred_element_type=jnp.float32)


def split_two(value):
    high = value.astype(jnp.bfloat16)
    low = (value - high.astype(jnp.float32)).astype(jnp.bfloat16)
    return high, low


def dense_kernel(
    shards,
    parts,
    base_ref,
    pooled_ref,
    *refs,
):
    weight_refs, refs = refs[:parts], refs[parts:]
    dense_body(shards, base_ref, pooled_ref, weight_refs, *refs)


def dense_body(
    shards,
    base_ref,
    pooled_ref,
    weight_refs,
    bias_ref,
    tower_bias_ref,
    head_ref,
    head_bias_ref,
    live_ref,
    label_ref,
    scale_ref,
    grad_ref,
    expert_grad_ref,
    x_ref,
    gate_grad_ref,
    tower_grad_ref,
    bias_grad_ref,
    small_ref,
    out_ref,
    slope_ref,
    tower_out_ref,
    spread_ref,
    total_ref,
    tower_ref,
    expand_ref,
    head_expand_ref,
):
    pairs = pooled_ref.shape[0]
    block = pooled_ref.shape[1]
    extra_ref = weight_refs[0].at[weight_refs[0].shape[0] - 1]
    in_first = weight_refs[0].shape[0] - 1
    depth = extra_ref.shape[0] // shards
    half = depth // 2
    step = pl.program_id(0)
    f32, bf16 = jnp.float32, jnp.bfloat16

    @pl.when(step == 0)
    def _():
        for i in range(shards):
            tower_ref[i * half : (i + 1) * half, :] = extra_ref[
                i * depth : i * depth + half, LANES : LANES + PACKED
            ]
        source = lax.broadcasted_iota(jnp.int32, (LANES, PACKED), 0)
        task = lax.broadcasted_iota(jnp.int32, (LANES, PACKED), 1) // TOWER
        head_expand_ref[...] = (source == task).astype(f32).astype(bf16)
        for e in range(EXPERTS):
            expert = (base_ref[0] + e) % EXPERTS
            expand_ref[e] = (source == task * EXPERTS + expert).astype(f32).astype(bf16)
        small_ref[...] = jnp.zeros_like(small_ref)
        tower_grad_ref[...] = jnp.zeros_like(tower_grad_ref)
        bias_grad_ref[...] = jnp.zeros_like(bias_grad_ref)

    left = left_lanes(block)
    for m in range(pairs // 2):
        even = pooled_ref[2 * m].astype(f32)
        odd = pooled_ref[2 * m + 1].astype(f32)
        low = jnp.where(left, even, pltpu.roll(odd, WIDTH, 1)).astype(bf16)
        high = jnp.where(left, pltpu.roll(even, WIDTH, 1), odd).astype(bf16)
        x_ref[:, m * LANES : (m + 1) * LANES] = low
        high_at = (m + pairs // 2) * LANES
        x_ref[:, high_at : high_at + LANES] = high

    def weight(e):
        return weight_refs[0][e] if e < in_first else weight_refs[1][e - in_first]

    logits = dot(x_ref[...], extra_ref[:, 0:LANES])
    powers = jnp.exp(logits - group_reduce(logits, jnp.maximum))
    gates = powers / group_reduce(powers, jnp.add)
    gates_high, gates_low = split_two(gates)

    total_ref[...] = jnp.zeros_like(total_ref)

    def expert(e, carry):
        pre = dot(x_ref[...], weight(e)) + bias_ref[e]
        sigma = jax.nn.sigmoid(pre)
        out = pre * sigma
        slope_ref[e] = sigma + out * (1.0 - sigma)
        out_low = out.astype(bf16)
        out_ref[e] = out_low
        product = dot(out_low, tower_ref[...])
        spread = dot(gates_high, expand_ref[e]) + dot(gates_low, expand_ref[e])
        tower_out_ref[e] = product
        spread_ref[e] = spread
        total_ref[...] += spread * product
        return carry

    loop(expert)

    pre = total_ref[...] + tower_bias_ref[...]
    sigma = jax.nn.sigmoid(pre)
    tower_out = pre * sigma
    slope = sigma + tower_out * (1.0 - sigma)
    high, low = split_two(tower_out * head_ref[...])
    logit = dot_nt(high, head_expand_ref[...]) + dot_nt(low, head_expand_ref[...])
    logit = logit + head_bias_ref[...]
    live = live_ref[...]
    label = label_ref[...]
    softplus = jnp.maximum(logit, 0.0) + jnp.log1p(jnp.exp(-jnp.abs(logit)))
    losses = live * (softplus - label * logit)
    logit_grad = live * (jax.nn.sigmoid(logit) - label) * scale_ref[0]
    high, low = split_two(logit_grad)
    signal = dot(high, head_expand_ref[...]) + dot(low, head_expand_ref[...])
    pre_grad = (signal * head_ref[...] * slope).astype(bf16).astype(f32)
    small_ref[0:1, :] += jnp.sum(signal * tower_out, axis=0, keepdims=True)
    small_ref[1:2, :] += jnp.sum(pre_grad, axis=0, keepdims=True)
    small_ref[2:3, 0:LANES] += jnp.sum(logit_grad, axis=0, keepdims=True)
    small_ref[3:4, 0:LANES] += jnp.sum(losses, axis=0, keepdims=True)

    total_ref[...] = pre_grad

    def back(e, carry):
        gate_prob, pooled_grad = carry
        pre_grad = total_ref[...]
        weighed = (spread_ref[e] * pre_grad).astype(bf16)
        tower_grad_ref[...] += dot_tn(weighed, out_ref[e])
        expert_grad = (dot_nt(weighed, tower_ref[...]) * slope_ref[e]).astype(bf16)
        expert_grad_ref[e] = expert_grad
        bias_grad_ref[e] += jnp.sum(expert_grad.astype(f32), axis=0, keepdims=True)
        high, low = split_two(tower_out_ref[e] * pre_grad)
        gate_prob = gate_prob + dot_nt(high, expand_ref[e]) + dot_nt(low, expand_ref[e])
        pooled_grad = pooled_grad + dot_nt(expert_grad, weight(e))
        return gate_prob, pooled_grad

    gate_prob, pooled_grad = loop(
        back, (jnp.zeros((block, LANES), f32), jnp.zeros((block, pairs * LANES), f32))
    )
    weighed = gates * gate_prob
    gate_grad = (weighed - gates * group_reduce(weighed, jnp.add)).astype(bf16)
    gate_grad_ref[...] = gate_grad
    pooled_grad = pooled_grad + dot_nt(gate_grad, extra_ref[:, 0:LANES])
    for m in range(pairs // 2):
        low = pooled_grad[:, m * LANES : (m + 1) * LANES]
        high_at = (m + pairs // 2) * LANES
        high = pooled_grad[:, high_at : high_at + LANES]
        grad_ref[2 * m] = jnp.where(left, low, pltpu.roll(high, WIDTH, 1))
        grad_ref[2 * m + 1] = jnp.where(left, pltpu.roll(low, WIDTH, 1), high)


def loop(body, carry=0):
    for e in range(EXPERTS):
        carry = body(e, carry)
    return carry


def dense(base, pooled, weights, bias, tower_bias, head, head_bias, live, label, scale, shards):
    pairs, samples = pooled.shape[:2]
    inner = weights[0].shape[1]
    slabs = [weights[0].shape[0], EXPERTS + 1 - weights[0].shape[0]][: len(weights)]
    block = 256
    whole = lambda *shape: pl.BlockSpec(
        shape, lambda i: (0,) * len(shape), pipeline_mode=pl.Buffered(1)
    )
    kept = lambda *shape: pl.BlockSpec(shape, lambda i: (0,) * len(shape))
    f32, bf16 = jnp.float32, jnp.bfloat16
    return pl.pallas_call(
        functools.partial(dense_kernel, shards, len(weights)),
        name="dense",
        grid=(samples // block,),
        in_specs=[
            pl.BlockSpec(memory_space=pltpu.SMEM),
            pl.BlockSpec((pairs, block, LANES), lambda i: (0, i, 0)),
        ]
        + [whole(n, inner, HID) for n in slabs]
        + [
            whole(EXPERTS, 1, HID),
            whole(1, PACKED),
            whole(1, PACKED),
            whole(1, LANES),
            pl.BlockSpec((block, LANES), lambda i: (i, 0)),
            pl.BlockSpec((block, LANES), lambda i: (i, 0)),
            pl.BlockSpec(memory_space=pltpu.SMEM),
        ],
        out_specs=[
            pl.BlockSpec((pairs, block, LANES), lambda i: (0, i, 0)),
            pl.BlockSpec((EXPERTS, block, HID), lambda i: (0, i, 0)),
            pl.BlockSpec((block, inner), lambda i: (i, 0)),
            pl.BlockSpec((block, LANES), lambda i: (i, 0)),
            kept(PACKED, HID),
            kept(EXPERTS, 1, HID),
            kept(8, PACKED),
        ],
        out_shape=[
            jax.ShapeDtypeStruct((pairs, samples, LANES), f32),
            jax.ShapeDtypeStruct((EXPERTS, samples, HID), bf16),
            jax.ShapeDtypeStruct((samples, inner), bf16),
            jax.ShapeDtypeStruct((samples, LANES), bf16),
            jax.ShapeDtypeStruct((PACKED, HID), f32),
            jax.ShapeDtypeStruct((EXPERTS, 1, HID), f32),
            jax.ShapeDtypeStruct((8, PACKED), f32),
        ],
        scratch_shapes=[
            pltpu.VMEM((EXPERTS, block, HID), bf16),
            pltpu.VMEM((EXPERTS, block, HID), f32),
            pltpu.VMEM((EXPERTS, block, PACKED), f32),
            pltpu.VMEM((EXPERTS, block, PACKED), f32),
            pltpu.VMEM((block, PACKED), f32),
            pltpu.VMEM((HID, PACKED), bf16),
            pltpu.VMEM((EXPERTS, LANES, PACKED), bf16),
            pltpu.VMEM((LANES, PACKED), bf16),
        ],
        compiler_params=params(),
        cost_estimate=cost(60),
    )(base, pooled, *weights, bias, tower_bias, head, head_bias, live, label, scale)


def weight_grad_kernel(
    shards, which_ref, x_ref, expert_ref, gate_ref, tower_ref, out_ref, extra_ref, turned_ref
):
    step = pl.program_id(0)
    last = pl.num_programs(0) - 1
    inner = x_ref.shape[1]
    depth = inner // shards
    half = depth // 2

    @pl.when(step == 0)
    def _():
        turned_ref[...] = x_ref[...].T

    @pl.when(step < last)
    def _():
        out_ref[0] = dot(turned_ref[...], expert_ref[0]).astype(jnp.bfloat16)

    @pl.when(step == last)
    def _():
        gate = dot(turned_ref[...], gate_ref[...])
        extra_ref[0, :, 0:LANES] = gate.astype(jnp.bfloat16)
        turned = tower_ref[...].T
        none = jnp.zeros((depth - half, PACKED), jnp.float32)
        runs = []
        for i in range(shards):
            runs += [turned[i * half : (i + 1) * half, :], none]
        extra_ref[0, :, LANES:] = jnp.concatenate(runs, axis=0).astype(jnp.bfloat16)


def weight_grads(which, x, expert_grad, gate_grad, tower_grad, shards):
    samples, inner = x.shape
    count = which.shape[0]
    whole = lambda *shape: pl.BlockSpec(
        shape, lambda i, w: (0,) * len(shape), pipeline_mode=pl.Buffered(1)
    )
    upto = lambda i: jnp.minimum(i, count - 1)
    return pl.pallas_call(
        functools.partial(weight_grad_kernel, shards),
        name="weight_grads",
        grid_spec=pltpu.PrefetchScalarGridSpec(
            num_scalar_prefetch=1,
            grid=(count + 1,),
            in_specs=[
                whole(samples, inner),
                pl.BlockSpec((1, samples, HID), lambda i, w: (w[upto(i)], 0, 0)),
                whole(samples, LANES),
                whole(PACKED, HID),
            ],
            out_specs=[
                pl.BlockSpec((1, inner, HID), lambda i, w: (upto(i), 0, 0)),
                pl.BlockSpec((1, inner, HID), lambda i, w: (0, 0, 0)),
            ],
            scratch_shapes=[pltpu.VMEM((inner, samples), jnp.bfloat16)],
        ),
        out_shape=[
            jax.ShapeDtypeStruct((count, inner, HID), jnp.bfloat16),
            jax.ShapeDtypeStruct((1, inner, HID), jnp.bfloat16),
        ],
        compiler_params=params(),
        cost_estimate=cost(18),
    )(which, x, expert_grad, gate_grad, tower_grad)


def order(value, *after):
    return pl.pallas_call(
        lambda *refs: None,
        name="order",
        in_specs=[ANYWHERE] * (1 + len(after)),
        out_specs=ANYWHERE,
        out_shape=jax.ShapeDtypeStruct(value.shape, value.dtype),
        input_output_aliases={0: 0},
    )(value, *after)


def dense_adam_kernel(part, rep_ref, here_ref, there_ref, more_ref, other_ref, *refs):
    expert, gate, tower = refs[0:3], refs[3:6], refs[6:9]
    expert_out, gate_out, tower_out = refs[9:12], refs[12:15], refs[15:18]
    step = pl.program_id(0)
    depth = more_ref.shape[1]
    half = depth // 2

    def put(outs, at, values):
        for out_ref, value in zip(outs, values):
            out_ref[at] = value

    grad = there_ref[0].astype(jnp.float32)
    if part < EXPERTS:
        mine = rep_ref[0] == step // part
        grad = jnp.where(mine, here_ref[0].astype(jnp.float32), grad)
    put(expert_out, 0, adamw(expert[0][0], grad, expert[1][0], expert[2][0], rate_expert))

    @pl.when(step == 0)
    def _():
        grad = more_ref[0].astype(jnp.float32) + other_ref[0].astype(jnp.float32)
        gate_grad = grad[:, 0:LANES].T[0 : TASKS * EXPERTS, :]
        put(gate_out, ..., adamw(gate[0][...], gate_grad, gate[1][...], gate[2][...], rate_gate))
        for k in range(TASKS):
            tower_grad = grad[0:half, LANES + k * TOWER : LANES + (k + 1) * TOWER]
            put(tower_out, k, adamw(tower[0][k], tower_grad, tower[1][k], tower[2][k], rate_tower))


def dense_adam(rep, here, there, extra, expert, gate, tower):
    part = here.shape[0]
    count, depth = expert[0].shape[:2]
    slab = lambda at: pl.BlockSpec((1, depth, HID), lambda i: (at(i), 0, 0))
    whole = lambda value: pl.BlockSpec(value.shape, lambda i: (0,) * value.ndim)
    arrays = [*expert, *gate, *tower]
    specs = [slab(lambda i: i)] * 3 + [whole(value) for value in arrays[3:]]
    outs = pl.pallas_call(
        functools.partial(dense_adam_kernel, part),
        name="dense_adam",
        grid=(count,),
        in_specs=[
            pl.BlockSpec(memory_space=pltpu.SMEM),
            slab(lambda i: i % part),
            slab(lambda i: i % part),
            slab(lambda i: extra[0].shape[0] - 1),
            slab(lambda i: extra[1].shape[0] - 1),
        ]
        + specs,
        out_specs=specs,
        out_shape=[jax.ShapeDtypeStruct(value.shape, jnp.float32) for value in arrays],
        compiler_params=params(),
    )(rep, here, there, *extra, *arrays)
    return outs[0:3], outs[3:6], outs[6:9]


def swap_rep(value):
    return lax.ppermute(value, "rep", [(0, 1), (1, 0)])


def sum_over(value, axis, first, last):
    size = lax.axis_size(axis)
    if size & (size - 1):
        return value if first else lax.psum(value, axis)
    shift = 1 << first
    while shift < min(size, 1 << last):
        value = value + lax.ppermute(value, axis, [(i, i ^ shift) for i in range(size)])
        shift *= 2
    return value


def pack_extra(gate, tower):
    depth = gate.shape[0]
    half = depth // 2
    side = jnp.transpose(tower, (1, 0, 2)).reshape(half, TASKS * TOWER)
    slab = jnp.pad(gate, ((0, 0), (0, HID - gate.shape[1])))
    return slab + jnp.pad(side, ((0, depth - half), (LANES, HID - LANES - TASKS * TOWER)))


def on_device(
    row_ids,
    bag_lengths,
    sample_counts,
    label_mask,
    labels,
    tables,
    table_m,
    table_v,
    expert_w,
    expert_m,
    expert_v,
    gate_w,
    gate_m,
    gate_v,
    tower_weight_matrix,
    tower_m,
    tower_v,
    small_params,
    small_m,
    small_v,
):
    shards = lax.axis_size("shard")
    reps = lax.axis_size("rep")
    rep = lax.axis_index("rep")
    device = rep * shards + lax.axis_index("shard")
    samples, bags, longest = row_ids.shape[:3]
    rows_dev = tables.shape[0]
    depth = gate_w.shape[0]
    half = depth // 2
    slots = samples * bags * longest
    capacity = slots // shards
    distinct = capacity // 4
    pairs = bags // TABLES
    int32 = jnp.int32
    both = range(TABLES)

    extra = pack_extra(gate_w, tower_weight_matrix)[None]
    if reps == 2:
        part = EXPERTS // 2
        base = rep * part
        line = jnp.arange(part, dtype=int32)
        chosen = jnp.where(rep == 0, expert_w[:part], expert_w[part:])
    else:
        base = jnp.zeros_like(rep)
        chosen = expert_w
    own = jnp.concatenate([chosen, extra], axis=0).astype(jnp.bfloat16)
    weights = [lax.all_gather(own, "shard", axis=1, tiled=True)]
    if reps == 2:
        weights += [swap_rep(weights[0][:part])]

    def by_slot(value):
        if reps != 2:
            return value
        turned = jnp.concatenate([value[part:], value[:part]], axis=0)
        return jnp.where(rep == 0, value, turned)

    def exchange(value):
        return lax.all_to_all(value, "shard", 0, 0, tiled=True)

    ids = jnp.transpose(row_ids, (1, 2, 3, 0))
    row = ids[:, :, 0, :] * ROW_BASE + ids[:, :, 1, :]
    lengths = jnp.transpose(bag_lengths)[:, None, :]
    number = lax.broadcasted_iota(int32, (pairs, longest, samples), 0) * longest
    place = lax.broadcasted_iota(int32, (pairs, longest, samples), 1)
    number = (number + place) * samples + lax.broadcasted_iota(int32, (pairs, longest, samples), 2)
    table_slots = pairs * longest * samples
    position = jnp.arange(table_slots, dtype=int32)
    span = table_slots
    wanted, grad_place, places = [], [], []
    for t in both:
        mine = slice(t * pairs, (t + 1) * pairs)
        payload = number + jnp.where(place >= lengths[mine], table_slots, 0)
        key, payload = lax.sort(
            (row[mine].reshape(table_slots), payload.reshape(table_slots)),
            num_keys=1,
            is_stable=False,
        )
        wanted.append(exchange((key % rows_dev).reshape(shards, 2 * distinct)).reshape(table_slots))
        skipped = payload >= table_slots
        slot = jnp.where(skipped, payload - table_slots, payload)
        bag = slot // (longest * samples)
        grad_place.append(
            jnp.where(skipped, pairs * samples, bag * samples + slot % samples)
        )
        reply_place = jnp.where(skipped, shards * distinct, position // 2)
        places.append(lax.sort(slot * span + reply_place, is_stable=False) % span)

    after = [[], places]
    found = [owner_gather(wanted[t], tables, after[t], shards, distinct, t) for t in both]
    replies = [exchange(value) for value in found]
    pooled = []
    for t in both:
        pooled = [pool(places[t], replies[t], pooled, samples, longest, pairs, t)]

    first_end = EXPERTS * HID
    second_end = first_end + TASKS * TOWER
    third_end = second_end + TASKS * TOWER
    fill = PACKED - TASKS * TOWER
    sample_total = jnp.sum(sample_counts).astype(jnp.float32)
    live_count = jnp.take(sample_counts, device)
    live = (jnp.arange(samples, dtype=int32) < live_count).astype(jnp.float32)[:, None]
    live = jnp.pad(live * label_mask.astype(jnp.float32), ((0, 0), (0, LANES - TASKS)))
    label = jnp.pad(labels.astype(jnp.float32), ((0, 0), (0, LANES - TASKS)))
    pooled_grad, expert_grad, x, gate_grad, tower_grad, bias_grad, sums = dense(
        base.astype(int32).reshape(1),
        pooled[0],
        weights,
        by_slot(small_params[:first_end].reshape(EXPERTS, 1, HID)),
        jnp.pad(small_params[first_end:second_end], (0, fill)).reshape(1, PACKED),
        jnp.pad(small_params[second_end:third_end], (0, fill)).reshape(1, PACKED),
        jnp.pad(small_params[third_end:], (0, LANES - TASKS)).reshape(1, LANES),
        live,
        label,
        (1.0 / sample_total).reshape(1),
        shards,
    )

    every = jnp.arange(EXPERTS, dtype=int32)
    kept, extra_grad = weight_grads(
        (every - base.astype(int32)) % EXPERTS, x, expert_grad, gate_grad, tower_grad, shards
    )
    if reps == 2:
        kept = lax.psum_scatter(kept, "rep", scatter_dimension=0, tiled=True)

    def owned_sum(value):
        return lax.psum_scatter(value, "shard", scatter_dimension=1, tiled=True)

    small_grad = jnp.concatenate(
        [
            by_slot(bias_grad).reshape(-1),
            sums[1, : TASKS * TOWER],
            sums[0, : TASKS * TOWER],
            sums[2, :TASKS],
            jnp.sum(sums[3, :TASKS]).reshape(1),
        ]
    )
    small_size = small_params.shape[0]
    padded = -(-(small_size + 1) // 1024) * 1024
    small_grad = jnp.pad(small_grad, (0, padded - small_size - 1))
    small_grad = small_grad.reshape(padded // LANES, LANES)
    pooled_grad = pooled_grad.reshape(pairs * samples, LANES)
    sent = []
    for t in both:
        sent.append(grad_gather(grad_place[t], pooled_grad, sent[:], shards, distinct, t))
    arrived = [exchange(value) for value in sent]
    chunks = (2, 2)
    table_parts = []
    after = [sent[1]]
    for t in both:
        mine = scatter(wanted[t], arrived[t], after, rows_dev, t, chunks[t])
        if reps == 2:
            table_parts.append([])
            for n, value in enumerate(mine):
                if t == 1:
                    value = order(value, (table_parts[0] + table_parts[1])[-1][1])
                table_parts[t].append((value, swap_rep(value)))
            after = [table_parts[0][0][1]]
        else:
            table_parts.append(
                [(lax.psum(v.astype(jnp.float32), "rep"), jnp.zeros_like(v)) for v in mine]
            )

    small_grad = order(small_grad, table_parts[1][0][0])
    small_grad = sum_over(small_grad, "shard", 0, 1)
    if reps == 2:
        table_parts[1][0] = (table_parts[1][0][0], order(table_parts[1][0][1], small_grad))
    table_state = []
    tokens = []
    for chunk, second_parts in enumerate(table_parts[1]):
        first_parts = table_parts[0][chunk * chunks[0] // chunks[1]]
        *table_state, token = table_adam(
            first_parts, second_parts, chunk, tables, table_m, table_v, table_state
        )
        tokens.append(token)
    table_new, table_m_new, table_v_new = table_state

    kept = jnp.concatenate([kept, extra_grad], axis=0)
    if reps == 2:
        kept = order(kept, arrived[1], table_parts[0][0][1])
    summed = owned_sum(kept)
    shard_bits = 2 if reps == 2 else 1
    expert = (expert_w, expert_m, expert_v)
    gate = [jnp.transpose(value) for value in (gate_w, gate_m, gate_v)]
    tower = (tower_weight_matrix, tower_m, tower_v)
    if reps == 2:
        summed = order(summed, tokens[-1])
        there = swap_rep(summed)
        small_grad = sum_over(order(small_grad, tokens[-1]), "shard", 1, 2)
        small_grad = order(small_grad, there)
        here = summed[:part]
        extra = (summed, there)
    else:
        here = lax.psum(summed.astype(jnp.float32), "rep")
        there = here
        extra = (here, jnp.zeros_like(here))
        here = here[:EXPERTS]
    expert_new, gate_new, tower_new = dense_adam(
        rep.astype(int32).reshape(1), here, there, extra, expert, gate, tower
    )
    expert_new, expert_m_new, expert_v_new = expert_new
    gate_new, gate_m_new, gate_v_new = [jnp.transpose(value) for value in gate_new]
    tower_new, tower_m_new, tower_v_new = tower_new
    small_sum = sum_over(sum_over(small_grad, "shard", shard_bits, 30), "rep", 0, 30).reshape(padded)
    small_new, small_m_new, small_v_new = adamw(
        small_params, small_sum[:small_size], small_m, small_v, rate_small
    )
    loss_parts = jnp.stack([small_sum[small_size], sample_total])
    return (
        loss_parts,
        table_new,
        table_m_new,
        table_v_new,
        expert_new,
        expert_m_new,
        expert_v_new,
        gate_new,
        gate_m_new,
        gate_v_new,
        tower_new,
        tower_m_new,
        tower_v_new,
        small_new,
        small_m_new,
        small_v_new,
    )


def solution(mesh):
    by_sample = ("rep", "shard")
    ins = (
        [P(by_sample, None, None, None), P(by_sample, None), P()]
        + [P(by_sample, None)] * 2
        + [P("shard", None)] * 3
        + [P(None, "shard", None)] * 3
        + [P("shard", None)] * 3
        + [P(None, "shard", None)] * 3
        + [P()] * 3
    )
    outs = (
        [P()]
        + [P("shard", None)] * 3
        + [P(None, "shard", None)] * 3
        + [P("shard", None)] * 3
        + [P(None, "shard", None)] * 3
        + [P()] * 3
    )
    return jax.shard_map(
        on_device, mesh=mesh, in_specs=tuple(ins), out_specs=tuple(outs), check_vma=False
    )
```

```python
import functools

import jax
import jax.numpy as jnp
from jax import lax
from jax.experimental import pallas as pl
from jax.experimental.pallas import tpu as pltpu
from jax.sharding import PartitionSpec as P

TABLES = 2
WIDTH = 64
ROW_BASE = 1024
EXPERTS = 8
HID = 512
TASKS = 5
TOWER = 64
STEP = 10
LANES = 128
UNROLL = 256
RMW = 8
PARTS = 8
PACKED = 3 * LANES
ANYWHERE = pl.BlockSpec(memory_space=pl.ANY)

beta_first = 0.9
beta_second = 0.999
adam_epsilon = 1e-08
weight_decay = 0.01
rate_table = 1.0
rate_expert = 0.06
rate_gate = 0.03
rate_tower = 0.08
rate_small = 0.5


def adamw(weight, grad, first, second, rate):
    first_new = beta_first * first + (1.0 - beta_first) * grad
    second_new = beta_second * second + (1.0 - beta_second) * grad * grad
    first_hat = first_new / (1.0 - beta_first**STEP)
    second_hat = second_new / (1.0 - beta_second**STEP)
    weight_new = weight - rate * (
        first_hat / (jnp.sqrt(second_hat) + adam_epsilon) + weight_decay * weight
    )
    return (weight_new, first_new, second_new)


def left_lanes(rows=1):
    return lax.broadcasted_iota(jnp.int32, (rows, LANES), 1) < WIDTH


def params(mebibytes=60):
    return pltpu.CompilerParams(vmem_limit_bytes=mebibytes << 20)


def pack(first, second, table):
    left = left_lanes(first.shape[0])
    if table == 0:
        return jnp.where(left, first, pltpu.roll(second, WIDTH, 1))
    return jnp.where(left, pltpu.roll(first, WIDTH, 1), second)


def unpack(value, table):
    turned = pltpu.roll(value, WIDTH, 1)
    return (value, turned) if table == 0 else (turned, value)


def cost(micros):
    return pl.CostEstimate(flops=0, bytes_accessed=int(micros * 1.0e2), transcendentals=0)


def owner_gather_kernel(distinct, table_at, want_ref, table_ref, *refs):
    out_ref, rows_ref = refs[-2:]

    def body(step, carry):
        base = step * UNROLL
        for u in range(UNROLL):
            rows_ref[pl.ds(base + u, 1), :] = table_ref[pl.ds(want_ref[2 * (base + u)], 1), :]
        return carry

    lax.fori_loop(0, distinct // UNROLL, body, 0)
    half = distinct // 2
    packed = pack(rows_ref[0:half, :], rows_ref[half:distinct, :], table_at)
    out_ref[0] = packed.astype(jnp.bfloat16)


def owner_gather(wanted, table, after, shards, distinct, table_at):
    rows = table.shape[0]
    return pl.pallas_call(
        functools.partial(owner_gather_kernel, distinct, table_at),
        name="owner_gather",
        grid=(shards,),
        in_specs=[
            pl.BlockSpec((2 * distinct,), lambda i: (i,), memory_space=pltpu.SMEM),
            pl.BlockSpec((rows, LANES), lambda i: (0, 0), pipeline_mode=pl.Buffered(1)),
        ]
        + [ANYWHERE] * len(after),
        out_specs=pl.BlockSpec((1, distinct // 2, LANES), lambda i: (i, 0, 0)),
        out_shape=jax.ShapeDtypeStruct((shards, distinct // 2, LANES), jnp.bfloat16),
        scratch_shapes=[pltpu.VMEM((distinct, LANES), jnp.float32)],
        compiler_params=params(),
        cost_estimate=cost(20),
    )(wanted, table, *after)


def pool_kernel(samples, longest, distinct, table_at, *refs):
    if table_at == 0:
        place_ref, reply_ref, out_ref, rows_ref, sum_ref = refs
    else:
        place_ref, reply_ref, before_ref, out_ref, rows_ref, sum_ref = refs
    shards, half = reply_ref.shape[:2]

    @pl.when(pl.program_id(0) == 0)
    def _():
        def spread(i, carry):
            first, second = unpack(reply_ref[i].astype(jnp.float32), table_at)
            base = pl.multiple_of(i * distinct, 8)
            rows_ref[pl.ds(base, half), :] = first
            rows_ref[pl.ds(base + half, half), :] = second
            return carry

        lax.fori_loop(0, shards, spread, 0)
        rows_ref[shards * distinct :, :] = jnp.zeros((8, LANES), jnp.float32)

    unroll = UNROLL // 4

    def body(step, carry):
        for u in range(unroll):
            s = step * unroll + u
            total = rows_ref[pl.ds(place_ref[s], 1), :]
            for slot in range(1, longest):
                total = total + rows_ref[pl.ds(place_ref[slot * samples + s], 1), :]
            sum_ref[pl.ds(s, 1), :] = total
        return carry

    lax.fori_loop(0, samples // unroll, body, 0)
    result = sum_ref[...]
    if table_at != 0:
        result = jnp.where(left_lanes(samples), before_ref[0].astype(jnp.float32), result)
    out_ref[0] = result.astype(jnp.bfloat16)


def pool(places, replies, before, samples, longest, pairs, table_at):
    shards, half = replies.shape[:2]
    distinct = 2 * half
    block = pl.BlockSpec((1, samples, LANES), lambda i: (i, 0, 0))
    return pl.pallas_call(
        functools.partial(pool_kernel, samples, longest, distinct, table_at),
        name="pool",
        grid=(pairs,),
        in_specs=[
            pl.BlockSpec(
                (longest * samples,), lambda i: (i + table_at * pairs,), memory_space=pltpu.SMEM
            ),
            pl.BlockSpec(memory_space=pltpu.VMEM),
        ]
        + [block] * len(before),
        out_specs=block,
        out_shape=jax.ShapeDtypeStruct((pairs, samples, LANES), jnp.bfloat16),
        scratch_shapes=[
            pltpu.VMEM((shards * distinct + 8, LANES), jnp.float32),
            pltpu.VMEM((samples, LANES), jnp.float32),
        ],
        compiler_params=params(20),
        cost_estimate=cost(30),
    )(places, replies, *before)


def grad_gather_kernel(distinct, table_at, index_ref, grad_ref, *refs):
    out_ref, grads_ref, rows_ref = refs[-3:]
    count = grad_ref.shape[0]

    @pl.when(pl.program_id(0) == 0)
    def _():
        grads_ref[0:count, :] = grad_ref[...]
        grads_ref[count : count + 8, :] = jnp.zeros((8, LANES), jnp.float32)

    unroll = UNROLL // 2

    def body(step, carry):
        for u in range(unroll):
            r = step * unroll + u
            first = grads_ref[pl.ds(index_ref[2 * r], 1), :]
            second = grads_ref[pl.ds(index_ref[2 * r + 1], 1), :]
            rows_ref[pl.ds(r, 1), :] = first + second
        return carry

    lax.fori_loop(0, distinct // unroll, body, 0)
    half = distinct // 2
    packed = pack(rows_ref[0:half, :], rows_ref[half:distinct, :], table_at)
    out_ref[0] = packed.astype(jnp.bfloat16)


def grad_gather(index, grads, after, shards, distinct, table_at):
    count = grads.shape[0]
    return pl.pallas_call(
        functools.partial(grad_gather_kernel, distinct, table_at),
        name="grad_gather",
        grid=(shards,),
        in_specs=[
            pl.BlockSpec((2 * distinct,), lambda i: (i,), memory_space=pltpu.SMEM),
            pl.BlockSpec((count, LANES), lambda i: (0, 0), pipeline_mode=pl.Buffered(1)),
        ]
        + [ANYWHERE] * len(after),
        out_specs=pl.BlockSpec((1, distinct // 2, LANES), lambda i: (i, 0, 0)),
        out_shape=jax.ShapeDtypeStruct((shards, distinct // 2, LANES), jnp.bfloat16),
        scratch_shapes=[
            pltpu.VMEM((count + 8, LANES), jnp.float32),
            pltpu.VMEM((distinct, LANES), jnp.float32),
        ],
        compiler_params=params(),
        cost_estimate=cost(32),
    )(index, grads, *after)


def scatter_kernel(distinct, table_at, outs, want0_ref, want1_ref, got_ref, *refs):
    out_refs, (sum0_ref, sum1_ref, rows_ref) = refs[-3 - outs : -3], refs[-3:]
    half = distinct // 2
    sums = (sum0_ref, sum1_ref)
    wants = (want0_ref, want1_ref)

    @pl.when(pl.program_id(0) == 0)
    def _():
        sum0_ref[...] = jnp.zeros_like(sum0_ref)
        sum1_ref[...] = jnp.zeros_like(sum1_ref)

    for i in range(2):
        first, second = unpack(got_ref[i].astype(jnp.float32), table_at)
        rows_ref[i, 0:half, :] = first
        rows_ref[i, half:distinct, :] = second

    def put(waiting):
        ref, places, values = waiting
        for place, value in zip(places, values):
            ref[pl.ds(place, 1), :] = value

    def body(step, carry):
        waiting = None
        for part in range(PARTS):
            base = (step * PARTS + part) * RMW
            for i in range(2):
                places = [wants[i][2 * (base + u)] for u in range(RMW)]
                values = [
                    sums[i][pl.ds(places[u], 1), :] + rows_ref[i, pl.ds(base + u, 1), :]
                    for u in range(RMW)
                ]
                if waiting is not None:
                    put(waiting)
                waiting = (sums[i], places, values)
        put(waiting)
        return carry

    lax.fori_loop(0, distinct // (RMW * PARTS), body, 0)

    @pl.when(pl.program_id(0) == pl.num_programs(0) - 1)
    def _():
        count = out_refs[0].shape[0]
        chunk = count // 8
        for n, out_ref in enumerate(out_refs):

            def finish(i, carry):
                low = pl.ds(pl.multiple_of(n * count + i * chunk, 16), chunk)
                high = pl.ds(pl.multiple_of((len(out_refs) + n) * count + i * chunk, 16), chunk)
                total = pack(
                    sum0_ref[low, :] + sum1_ref[low, :],
                    sum0_ref[high, :] + sum1_ref[high, :],
                    table_at,
                )
                out_ref[pl.ds(pl.multiple_of(i * chunk, 16), chunk), :] = total.astype(jnp.bfloat16)
                return carry

            lax.fori_loop(0, 8, finish, 0)


def scatter(wanted, arrived, after, rows, table_at, outs):
    shards, half = arrived.shape[:2]
    distinct = 2 * half
    want = lambda j: pl.BlockSpec(
        (2 * distinct,), lambda i: (2 * i + j,), memory_space=pltpu.SMEM
    )
    count = rows // 2 // outs
    return pl.pallas_call(
        functools.partial(scatter_kernel, distinct, table_at, outs),
        name="scatter",
        grid=(shards // 2,),
        in_specs=[
            want(0),
            want(1),
            pl.BlockSpec((2, half, LANES), lambda i: (i, 0, 0)),
        ]
        + [ANYWHERE] * len(after),
        out_specs=[pl.BlockSpec((count, LANES), lambda i: (0, 0))] * outs,
        out_shape=[jax.ShapeDtypeStruct((count, LANES), jnp.bfloat16)] * outs,
        scratch_shapes=[
            pltpu.VMEM((rows, LANES), jnp.float32),
            pltpu.VMEM((rows, LANES), jnp.float32),
            pltpu.VMEM((2, distinct, LANES), jnp.float32),
        ],
        compiler_params=params(36),
        cost_estimate=cost(24),
    )(wanted, wanted, arrived, *after)


def table_adam_kernel(*refs):
    parts = refs[:4]
    weight_ref, first_ref, second_ref = refs[4:7]
    weight_out, first_out, second_out, token_ref = refs[-4:]
    later = pl.program_id(0) >= pl.num_programs(0) // 2
    sum0 = parts[0][...].astype(jnp.float32) + parts[1][...].astype(jnp.float32)
    sum1 = parts[2][...].astype(jnp.float32) + parts[3][...].astype(jnp.float32)
    left = left_lanes(sum0.shape[0])
    early_grad = jnp.where(left, sum0, pltpu.roll(sum1, WIDTH, 1))
    late_grad = jnp.where(left, pltpu.roll(sum0, WIDTH, 1), sum1)
    grad = jnp.where(later, late_grad, early_grad)
    weight, first, second = adamw(
        weight_ref[...], grad, first_ref[...], second_ref[...], rate_table
    )
    weight_out[...] = weight
    first_out[...] = first
    second_out[...] = second
    token_ref[...] = jnp.zeros_like(token_ref)


def table_adam(first_parts, second_parts, chunk, weight, first, second, before):
    rows = weight.shape[0]
    count = second_parts[0].shape[0]
    block = min(1024, count)
    steps = count // block
    full_at = lambda i: (chunk * steps + i % steps + i // steps * (rows // 2 // block), 0)
    inside = chunk * count % first_parts[0].shape[0] // block
    early = pl.BlockSpec((block, LANES), lambda i: (inside + i % steps, 0))
    packed = pl.BlockSpec((block, LANES), lambda i: (i % steps, 0))
    full = pl.BlockSpec((block, LANES), full_at)
    return pl.pallas_call(
        table_adam_kernel,
        name="table_adam",
        grid=(2 * steps,),
        in_specs=[early] * 2
        + [packed] * 2
        + [full] * 3
        + [pl.BlockSpec(memory_space=pl.ANY)] * len(before),
        out_specs=[full] * 3 + [pl.BlockSpec((8, LANES), lambda i: (0, 0))],
        out_shape=[jax.ShapeDtypeStruct(weight.shape, jnp.float32)] * 3
        + [jax.ShapeDtypeStruct((8, LANES), jnp.float32)],
        input_output_aliases={7 + i: i for i in range(len(before))},
        compiler_params=params(),
        cost_estimate=cost(7),
    )(*first_parts, *second_parts, weight, first, second, *before)


def group_reduce(value, op):
    lane = lax.broadcasted_iota(jnp.int32, value.shape, 1)
    shift = 1
    while shift < EXPERTS:
        other = jnp.where(
            (lane & shift) != 0,
            pltpu.roll(value, shift, 1),
            pltpu.roll(value, LANES - shift, 1),
        )
        value = op(value, other)
        shift *= 2
    return value


def dot(a, b):
    return jnp.dot(a, b, preferred_element_type=jnp.float32)


def dot_nt(a, b):
    return lax.dot_general(a, b, (((1,), (1,)), ((), ())), preferred_element_type=jnp.float32)


def dot_tn(a, b):
    return lax.dot_general(a, b, (((0,), (0,)), ((), ())), preferred_element_type=jnp.float32)


def split_two(value):
    high = value.astype(jnp.bfloat16)
    low = (value - high.astype(jnp.float32)).astype(jnp.bfloat16)
    return high, low


def dense_kernel(
    shards,
    parts,
    base_ref,
    pooled_ref,
    *refs,
):
    weight_refs, refs = refs[:parts], refs[parts:]
    dense_body(shards, base_ref, pooled_ref, weight_refs, *refs)


def dense_body(
    shards,
    base_ref,
    pooled_ref,
    weight_refs,
    bias_ref,
    tower_bias_ref,
    head_ref,
    head_bias_ref,
    live_ref,
    label_ref,
    scale_ref,
    grad_ref,
    expert_grad_ref,
    x_ref,
    gate_grad_ref,
    tower_grad_ref,
    bias_grad_ref,
    small_ref,
    out_ref,
    slope_ref,
    tower_out_ref,
    spread_ref,
    total_ref,
    tower_ref,
    expand_ref,
    head_expand_ref,
):
    pairs = pooled_ref.shape[0]
    block = pooled_ref.shape[1]
    extra_ref = weight_refs[0].at[weight_refs[0].shape[0] - 1]
    in_first = weight_refs[0].shape[0] - 1
    depth = extra_ref.shape[0] // shards
    half = depth // 2
    step = pl.program_id(0)
    f32, bf16 = jnp.float32, jnp.bfloat16

    @pl.when(step == 0)
    def _():
        for i in range(shards):
            tower_ref[i * half : (i + 1) * half, :] = extra_ref[
                i * depth : i * depth + half, LANES : LANES + PACKED
            ]
        source = lax.broadcasted_iota(jnp.int32, (LANES, PACKED), 0)
        task = lax.broadcasted_iota(jnp.int32, (LANES, PACKED), 1) // TOWER
        head_expand_ref[...] = (source == task).astype(f32).astype(bf16)
        for e in range(EXPERTS):
            expert = (base_ref[0] + e) % EXPERTS
            expand_ref[e] = (source == task * EXPERTS + expert).astype(f32).astype(bf16)
        small_ref[...] = jnp.zeros_like(small_ref)
        tower_grad_ref[...] = jnp.zeros_like(tower_grad_ref)
        bias_grad_ref[...] = jnp.zeros_like(bias_grad_ref)

    left = left_lanes(block)
    for m in range(pairs // 2):
        even = pooled_ref[2 * m].astype(f32)
        odd = pooled_ref[2 * m + 1].astype(f32)
        low = jnp.where(left, even, pltpu.roll(odd, WIDTH, 1)).astype(bf16)
        high = jnp.where(left, pltpu.roll(even, WIDTH, 1), odd).astype(bf16)
        x_ref[:, m * LANES : (m + 1) * LANES] = low
        high_at = (m + pairs // 2) * LANES
        x_ref[:, high_at : high_at + LANES] = high

    def weight(e):
        return weight_refs[0][e] if e < in_first else weight_refs[1][e - in_first]

    logits = dot(x_ref[...], extra_ref[:, 0:LANES])
    powers = jnp.exp(logits - group_reduce(logits, jnp.maximum))
    gates = powers / group_reduce(powers, jnp.add)
    gates_high, gates_low = split_two(gates)

    total_ref[...] = jnp.zeros_like(total_ref)

    def expert(e, carry):
        pre = dot(x_ref[...], weight(e)) + bias_ref[e]
        sigma = jax.nn.sigmoid(pre)
        out = pre * sigma
        slope_ref[e] = (sigma + out * (1.0 - sigma)).astype(bf16)
        out_low = out.astype(bf16)
        out_ref[e] = out_low
        product = dot(out_low, tower_ref[...])
        spread = dot(gates_high, expand_ref[e]) + dot(gates_low, expand_ref[e])
        tower_out_ref[e] = product
        spread_ref[e] = spread
        total_ref[...] += spread * product
        return carry

    loop(expert)

    pre = total_ref[...] + tower_bias_ref[...]
    sigma = jax.nn.sigmoid(pre)
    tower_out = pre * sigma
    slope = sigma + tower_out * (1.0 - sigma)
    high, low = split_two(tower_out * head_ref[...])
    logit = dot_nt(high, head_expand_ref[...]) + dot_nt(low, head_expand_ref[...])
    logit = logit + head_bias_ref[...]
    live = live_ref[...]
    label = label_ref[...]
    softplus = jnp.maximum(logit, 0.0) + jnp.log1p(jnp.exp(-jnp.abs(logit)))
    losses = live * (softplus - label * logit)
    logit_grad = live * (jax.nn.sigmoid(logit) - label) * scale_ref[0]
    high, low = split_two(logit_grad)
    signal = dot(high, head_expand_ref[...]) + dot(low, head_expand_ref[...])
    pre_grad = (signal * head_ref[...] * slope).astype(bf16).astype(f32)
    small_ref[0:1, :] += jnp.sum(signal * tower_out, axis=0, keepdims=True)
    small_ref[1:2, :] += jnp.sum(pre_grad, axis=0, keepdims=True)
    small_ref[2:3, 0:LANES] += jnp.sum(logit_grad, axis=0, keepdims=True)
    small_ref[3:4, 0:LANES] += jnp.sum(losses, axis=0, keepdims=True)

    total_ref[...] = pre_grad

    def back(e, carry):
        gate_prob, pooled_grad = carry
        pre_grad = total_ref[...]
        weighed = (spread_ref[e] * pre_grad).astype(bf16)
        tower_grad_ref[...] += dot_tn(weighed, out_ref[e])
        expert_grad = (dot_nt(weighed, tower_ref[...]) * slope_ref[e]).astype(bf16)
        expert_grad_ref[e] = expert_grad
        bias_grad_ref[e] += jnp.sum(expert_grad.astype(f32), axis=0, keepdims=True)
        high, low = split_two(tower_out_ref[e] * pre_grad)
        gate_prob = gate_prob + dot_nt(high, expand_ref[e]) + dot_nt(low, expand_ref[e])
        pooled_grad = pooled_grad + dot_nt(expert_grad, weight(e))
        return gate_prob, pooled_grad

    gate_prob, pooled_grad = loop(
        back, (jnp.zeros((block, LANES), f32), jnp.zeros((block, pairs * LANES), f32))
    )
    weighed = gates * gate_prob
    gate_grad = (weighed - gates * group_reduce(weighed, jnp.add)).astype(bf16)
    gate_grad_ref[...] = gate_grad
    pooled_grad = pooled_grad + dot_nt(gate_grad, extra_ref[:, 0:LANES])
    for m in range(pairs // 2):
        low = pooled_grad[:, m * LANES : (m + 1) * LANES]
        high_at = (m + pairs // 2) * LANES
        high = pooled_grad[:, high_at : high_at + LANES]
        grad_ref[2 * m] = jnp.where(left, low, pltpu.roll(high, WIDTH, 1))
        grad_ref[2 * m + 1] = jnp.where(left, pltpu.roll(low, WIDTH, 1), high)


def loop(body, carry=0):
    for e in range(EXPERTS):
        carry = body(e, carry)
    return carry


def dense(base, pooled, weights, bias, tower_bias, head, head_bias, live, label, scale, shards):
    pairs, samples = pooled.shape[:2]
    inner = weights[0].shape[1]
    slabs = [weights[0].shape[0], EXPERTS + 1 - weights[0].shape[0]][: len(weights)]
    block = 512
    whole = lambda *shape: pl.BlockSpec(
        shape, lambda i: (0,) * len(shape), pipeline_mode=pl.Buffered(1)
    )
    kept = lambda *shape: pl.BlockSpec(shape, lambda i: (0,) * len(shape))
    f32, bf16 = jnp.float32, jnp.bfloat16
    return pl.pallas_call(
        functools.partial(dense_kernel, shards, len(weights)),
        name="dense",
        grid=(samples // block,),
        in_specs=[
            pl.BlockSpec(memory_space=pltpu.SMEM),
            pl.BlockSpec((pairs, block, LANES), lambda i: (0, i, 0)),
        ]
        + [whole(n, inner, HID) for n in slabs]
        + [
            whole(EXPERTS, 1, HID),
            whole(1, PACKED),
            whole(1, PACKED),
            whole(1, LANES),
            pl.BlockSpec((block, LANES), lambda i: (i, 0)),
            pl.BlockSpec((block, LANES), lambda i: (i, 0)),
            pl.BlockSpec(memory_space=pltpu.SMEM),
        ],
        out_specs=[
            pl.BlockSpec((pairs, block, LANES), lambda i: (0, i, 0)),
            pl.BlockSpec((EXPERTS, block, HID), lambda i: (0, i, 0)),
            pl.BlockSpec((block, inner), lambda i: (i, 0)),
            pl.BlockSpec((block, LANES), lambda i: (i, 0)),
            kept(PACKED, HID),
            kept(EXPERTS, 1, HID),
            kept(8, PACKED),
        ],
        out_shape=[
            jax.ShapeDtypeStruct((pairs, samples, LANES), f32),
            jax.ShapeDtypeStruct((EXPERTS, samples, HID), bf16),
            jax.ShapeDtypeStruct((samples, inner), bf16),
            jax.ShapeDtypeStruct((samples, LANES), bf16),
            jax.ShapeDtypeStruct((PACKED, HID), f32),
            jax.ShapeDtypeStruct((EXPERTS, 1, HID), f32),
            jax.ShapeDtypeStruct((8, PACKED), f32),
        ],
        scratch_shapes=[
            pltpu.VMEM((EXPERTS, block, HID), bf16),
            pltpu.VMEM((EXPERTS, block, HID), bf16),
            pltpu.VMEM((EXPERTS, block, PACKED), f32),
            pltpu.VMEM((EXPERTS, block, PACKED), f32),
            pltpu.VMEM((block, PACKED), f32),
            pltpu.VMEM((HID, PACKED), bf16),
            pltpu.VMEM((EXPERTS, LANES, PACKED), bf16),
            pltpu.VMEM((LANES, PACKED), bf16),
        ],
        compiler_params=params(),
        cost_estimate=cost(60),
    )(base, pooled, *weights, bias, tower_bias, head, head_bias, live, label, scale)


def weight_grad_kernel(
    shards, which_ref, x_ref, expert_ref, gate_ref, tower_ref, out_ref, extra_ref, turned_ref
):
    step = pl.program_id(0)
    last = pl.num_programs(0) - 1
    inner = x_ref.shape[1]
    depth = inner // shards
    half = depth // 2

    @pl.when(step == 0)
    def _():
        turned_ref[...] = x_ref[...].T

    @pl.when(step < last)
    def _():
        out_ref[0] = dot(turned_ref[...], expert_ref[0]).astype(jnp.bfloat16)

    @pl.when(step == last)
    def _():
        gate = dot(turned_ref[...], gate_ref[...])
        extra_ref[0, :, 0:LANES] = gate.astype(jnp.bfloat16)
        turned = tower_ref[...].T
        none = jnp.zeros((depth - half, PACKED), jnp.float32)
        runs = []
        for i in range(shards):
            runs += [turned[i * half : (i + 1) * half, :], none]
        extra_ref[0, :, LANES:] = jnp.concatenate(runs, axis=0).astype(jnp.bfloat16)


def weight_grads(which, x, expert_grad, gate_grad, tower_grad, shards):
    samples, inner = x.shape
    count = which.shape[0]
    whole = lambda *shape: pl.BlockSpec(
        shape, lambda i, w: (0,) * len(shape), pipeline_mode=pl.Buffered(1)
    )
    upto = lambda i: jnp.minimum(i, count - 1)
    return pl.pallas_call(
        functools.partial(weight_grad_kernel, shards),
        name="weight_grads",
        grid_spec=pltpu.PrefetchScalarGridSpec(
            num_scalar_prefetch=1,
            grid=(count + 1,),
            in_specs=[
                whole(samples, inner),
                pl.BlockSpec((1, samples, HID), lambda i, w: (w[upto(i)], 0, 0)),
                whole(samples, LANES),
                whole(PACKED, HID),
            ],
            out_specs=[
                pl.BlockSpec((1, inner, HID), lambda i, w: (upto(i), 0, 0)),
                pl.BlockSpec((1, inner, HID), lambda i, w: (0, 0, 0)),
            ],
            scratch_shapes=[pltpu.VMEM((inner, samples), jnp.bfloat16)],
        ),
        out_shape=[
            jax.ShapeDtypeStruct((count, inner, HID), jnp.bfloat16),
            jax.ShapeDtypeStruct((1, inner, HID), jnp.bfloat16),
        ],
        compiler_params=params(),
        cost_estimate=cost(18),
    )(which, x, expert_grad, gate_grad, tower_grad)


def order(value, *after):
    return pl.pallas_call(
        lambda *refs: None,
        name="order",
        in_specs=[ANYWHERE] * (1 + len(after)),
        out_specs=ANYWHERE,
        out_shape=jax.ShapeDtypeStruct(value.shape, value.dtype),
        input_output_aliases={0: 0},
    )(value, *after)


def dense_adam_kernel(part, rep_ref, here_ref, there_ref, more_ref, other_ref, *refs):
    expert, gate, tower = refs[0:3], refs[3:6], refs[6:9]
    expert_out, gate_out, tower_out = refs[9:12], refs[12:15], refs[15:18]
    step = pl.program_id(0)
    depth = more_ref.shape[1]
    half = depth // 2

    def put(outs, at, values):
        for out_ref, value in zip(outs, values):
            out_ref[at] = value

    grad = there_ref[0].astype(jnp.float32)
    if part < EXPERTS:
        mine = rep_ref[0] == step // part
        grad = jnp.where(mine, here_ref[0].astype(jnp.float32), grad)
    put(expert_out, 0, adamw(expert[0][0], grad, expert[1][0], expert[2][0], rate_expert))

    @pl.when(step == 0)
    def _():
        grad = more_ref[0].astype(jnp.float32) + other_ref[0].astype(jnp.float32)
        gate_grad = grad[:, 0:LANES].T[0 : TASKS * EXPERTS, :]
        put(gate_out, ..., adamw(gate[0][...], gate_grad, gate[1][...], gate[2][...], rate_gate))
        for k in range(TASKS):
            tower_grad = grad[0:half, LANES + k * TOWER : LANES + (k + 1) * TOWER]
            put(tower_out, k, adamw(tower[0][k], tower_grad, tower[1][k], tower[2][k], rate_tower))


def dense_adam(rep, here, there, extra, expert, gate, tower):
    part = here.shape[0]
    count, depth = expert[0].shape[:2]
    slab = lambda at: pl.BlockSpec((1, depth, HID), lambda i: (at(i), 0, 0))
    whole = lambda value: pl.BlockSpec(value.shape, lambda i: (0,) * value.ndim)
    arrays = [*expert, *gate, *tower]
    specs = [slab(lambda i: i)] * 3 + [whole(value) for value in arrays[3:]]
    outs = pl.pallas_call(
        functools.partial(dense_adam_kernel, part),
        name="dense_adam",
        grid=(count,),
        in_specs=[
            pl.BlockSpec(memory_space=pltpu.SMEM),
            slab(lambda i: i % part),
            slab(lambda i: i % part),
            slab(lambda i: extra[0].shape[0] - 1),
            slab(lambda i: extra[1].shape[0] - 1),
        ]
        + specs,
        out_specs=specs,
        out_shape=[jax.ShapeDtypeStruct(value.shape, jnp.float32) for value in arrays],
        compiler_params=params(),
    )(rep, here, there, *extra, *arrays)
    return outs[0:3], outs[3:6], outs[6:9]


def swap_rep(value):
    return lax.ppermute(value, "rep", [(0, 1), (1, 0)])


def sum_over(value, axis, first, last):
    size = lax.axis_size(axis)
    if size & (size - 1):
        return value if first else lax.psum(value, axis)
    shift = 1 << first
    while shift < min(size, 1 << last):
        value = value + lax.ppermute(value, axis, [(i, i ^ shift) for i in range(size)])
        shift *= 2
    return value


def pack_extra(gate, tower):
    depth = gate.shape[0]
    half = depth // 2
    side = jnp.transpose(tower, (1, 0, 2)).reshape(half, TASKS * TOWER)
    slab = jnp.pad(gate, ((0, 0), (0, HID - gate.shape[1])))
    return slab + jnp.pad(side, ((0, depth - half), (LANES, HID - LANES - TASKS * TOWER)))


def on_device(
    row_ids,
    bag_lengths,
    sample_counts,
    label_mask,
    labels,
    tables,
    table_m,
    table_v,
    expert_w,
    expert_m,
    expert_v,
    gate_w,
    gate_m,
    gate_v,
    tower_weight_matrix,
    tower_m,
    tower_v,
    small_params,
    small_m,
    small_v,
):
    shards = lax.axis_size("shard")
    reps = lax.axis_size("rep")
    rep = lax.axis_index("rep")
    device = rep * shards + lax.axis_index("shard")
    samples, bags, longest = row_ids.shape[:3]
    rows_dev = tables.shape[0]
    depth = gate_w.shape[0]
    half = depth // 2
    slots = samples * bags * longest
    capacity = slots // shards
    distinct = capacity // 4
    pairs = bags // TABLES
    int32 = jnp.int32
    both = range(TABLES)

    extra = pack_extra(gate_w, tower_weight_matrix)[None]
    if reps == 2:
        part = EXPERTS // 2
        base = rep * part
        line = jnp.arange(part, dtype=int32)
        chosen = jnp.where(rep == 0, expert_w[:part], expert_w[part:])
    else:
        base = jnp.zeros_like(rep)
        chosen = expert_w
    own = jnp.concatenate([chosen, extra], axis=0).astype(jnp.bfloat16)
    weights = [lax.all_gather(own, "shard", axis=1, tiled=True)]
    if reps == 2:
        weights += [swap_rep(weights[0][:part])]

    def by_slot(value):
        if reps != 2:
            return value
        turned = jnp.concatenate([value[part:], value[:part]], axis=0)
        return jnp.where(rep == 0, value, turned)

    def exchange(value):
        return lax.all_to_all(value, "shard", 0, 0, tiled=True)

    ids = jnp.transpose(row_ids, (1, 2, 3, 0))
    row = ids[:, :, 0, :] * ROW_BASE + ids[:, :, 1, :]
    lengths = jnp.transpose(bag_lengths)[:, None, :]
    number = lax.broadcasted_iota(int32, (pairs, longest, samples), 0) * longest
    place = lax.broadcasted_iota(int32, (pairs, longest, samples), 1)
    number = (number + place) * samples + lax.broadcasted_iota(int32, (pairs, longest, samples), 2)
    table_slots = pairs * longest * samples
    position = jnp.arange(table_slots, dtype=int32)
    span = table_slots
    wanted, grad_place, inverse = [], [], []
    for t in both:
        mine = slice(t * pairs, (t + 1) * pairs)
        payload = number + jnp.where(place >= lengths[mine], table_slots, 0)
        key, payload = lax.sort(
            (row[mine].reshape(table_slots), payload.reshape(table_slots)),
            num_keys=1,
            is_stable=False,
        )
        wanted.append(exchange((key % rows_dev).reshape(shards, 2 * distinct)).reshape(table_slots))
        skipped = payload >= table_slots
        slot = jnp.where(skipped, payload - table_slots, payload)
        bag = slot // (longest * samples)
        grad_place.append(
            jnp.where(skipped, pairs * samples, bag * samples + slot % samples)
        )
        reply_place = jnp.where(skipped, shards * distinct, position // 2)
        inverse.append((slot + t * table_slots) * span + reply_place)
    places = lax.sort(jnp.concatenate(inverse), is_stable=False) % span

    after = [[], [places]]
    found = [owner_gather(wanted[t], tables, after[t], shards, distinct, t) for t in both]
    replies = [exchange(value) for value in found]
    pooled = []
    for t in both:
        pooled = [pool(places, replies[t], pooled, samples, longest, pairs, t)]

    first_end = EXPERTS * HID
    second_end = first_end + TASKS * TOWER
    third_end = second_end + TASKS * TOWER
    fill = PACKED - TASKS * TOWER
    sample_total = jnp.sum(sample_counts).astype(jnp.float32)
    live_count = jnp.take(sample_counts, device)
    live = (jnp.arange(samples, dtype=int32) < live_count).astype(jnp.float32)[:, None]
    live = jnp.pad(live * label_mask.astype(jnp.float32), ((0, 0), (0, LANES - TASKS)))
    label = jnp.pad(labels.astype(jnp.float32), ((0, 0), (0, LANES - TASKS)))
    pooled_grad, expert_grad, x, gate_grad, tower_grad, bias_grad, sums = dense(
        base.astype(int32).reshape(1),
        pooled[0],
        weights,
        by_slot(small_params[:first_end].reshape(EXPERTS, 1, HID)),
        jnp.pad(small_params[first_end:second_end], (0, fill)).reshape(1, PACKED),
        jnp.pad(small_params[second_end:third_end], (0, fill)).reshape(1, PACKED),
        jnp.pad(small_params[third_end:], (0, LANES - TASKS)).reshape(1, LANES),
        live,
        label,
        (1.0 / sample_total).reshape(1),
        shards,
    )

    every = jnp.arange(EXPERTS, dtype=int32)
    kept, extra_grad = weight_grads(
        (every - base.astype(int32)) % EXPERTS, x, expert_grad, gate_grad, tower_grad, shards
    )
    if reps == 2:
        kept = lax.psum_scatter(kept, "rep", scatter_dimension=0, tiled=True)

    def owned_sum(value):
        return lax.psum_scatter(value, "shard", scatter_dimension=1, tiled=True)

    small_grad = jnp.concatenate(
        [
            by_slot(bias_grad).reshape(-1),
            sums[1, : TASKS * TOWER],
            sums[0, : TASKS * TOWER],
            sums[2, :TASKS],
            jnp.sum(sums[3, :TASKS]).reshape(1),
        ]
    )
    small_size = small_params.shape[0]
    padded = -(-(small_size + 1) // 1024) * 1024
    small_grad = jnp.pad(small_grad, (0, padded - small_size - 1))
    small_grad = small_grad.reshape(padded // LANES, LANES)
    pooled_grad = pooled_grad.reshape(pairs * samples, LANES)
    sent = []
    for t in both:
        sent.append(grad_gather(grad_place[t], pooled_grad, sent[:], shards, distinct, t))
    arrived = [exchange(value) for value in sent]
    chunks = (2, 2)
    table_parts = []
    after = [sent[1]]
    for t in both:
        mine = scatter(wanted[t], arrived[t], after, rows_dev, t, chunks[t])
        if reps == 2:
            table_parts.append([])
            for n, value in enumerate(mine):
                if t == 1:
                    value = order(value, (table_parts[0] + table_parts[1])[-1][1])
                table_parts[t].append((value, swap_rep(value)))
            after = [table_parts[0][0][1]]
        else:
            table_parts.append(
                [(lax.psum(v.astype(jnp.float32), "rep"), jnp.zeros_like(v)) for v in mine]
            )

    small_grad = order(small_grad, table_parts[1][0][0])
    small_grad = sum_over(small_grad, "shard", 0, 1)
    if reps == 2:
        table_parts[1][0] = (table_parts[1][0][0], order(table_parts[1][0][1], small_grad))
    table_state = []
    tokens = []
    for chunk, second_parts in enumerate(table_parts[1]):
        first_parts = table_parts[0][chunk * chunks[0] // chunks[1]]
        *table_state, token = table_adam(
            first_parts, second_parts, chunk, tables, table_m, table_v, table_state
        )
        tokens.append(token)
    table_new, table_m_new, table_v_new = table_state

    kept = jnp.concatenate([kept, extra_grad], axis=0)
    if reps == 2:
        kept = order(kept, arrived[1], table_parts[0][0][1])
    summed = owned_sum(kept)
    shard_bits = 3 if reps == 2 else 1
    expert = (expert_w, expert_m, expert_v)
    gate = [jnp.transpose(value) for value in (gate_w, gate_m, gate_v)]
    tower = (tower_weight_matrix, tower_m, tower_v)
    if reps == 2:
        summed = order(summed, tokens[-1])
        there = swap_rep(summed)
        small_grad = sum_over(order(small_grad, tokens[-1]), "shard", 1, 3)
        small_grad = order(small_grad, there)
        here = summed[:part]
        extra = (summed, there)
    else:
        here = lax.psum(summed.astype(jnp.float32), "rep")
        there = here
        extra = (here, jnp.zeros_like(here))
        here = here[:EXPERTS]
    expert_new, gate_new, tower_new = dense_adam(
        rep.astype(int32).reshape(1), here, there, extra, expert, gate, tower
    )
    expert_new, expert_m_new, expert_v_new = expert_new
    gate_new, gate_m_new, gate_v_new = [jnp.transpose(value) for value in gate_new]
    tower_new, tower_m_new, tower_v_new = tower_new
    small_sum = sum_over(sum_over(small_grad, "shard", shard_bits, 30), "rep", 0, 30).reshape(padded)
    small_new, small_m_new, small_v_new = adamw(
        small_params, small_sum[:small_size], small_m, small_v, rate_small
    )
    loss_parts = jnp.stack([small_sum[small_size], sample_total])
    return (
        loss_parts,
        table_new,
        table_m_new,
        table_v_new,
        expert_new,
        expert_m_new,
        expert_v_new,
        gate_new,
        gate_m_new,
        gate_v_new,
        tower_new,
        tower_m_new,
        tower_v_new,
        small_new,
        small_m_new,
        small_v_new,
    )


def solution(mesh):
    by_sample = ("rep", "shard")
    ins = (
        [P(by_sample, None, None, None), P(by_sample, None), P()]
        + [P(by_sample, None)] * 2
        + [P("shard", None)] * 3
        + [P(None, "shard", None)] * 3
        + [P("shard", None)] * 3
        + [P(None, "shard", None)] * 3
        + [P()] * 3
    )
    outs = (
        [P()]
        + [P("shard", None)] * 3
        + [P(None, "shard", None)] * 3
        + [P("shard", None)] * 3
        + [P(None, "shard", None)] * 3
        + [P()] * 3
    )
    return jax.shard_map(
        on_device, mesh=mesh, in_specs=tuple(ins), out_specs=tuple(outs), check_vma=False
    )
```
